256 devices in a mesh: rng: 32 (over x, y, core), dop: 8 (over z).
Axes of the slice: x: 4, y: 4, z: 8, core: 2. Of those that a mesh axis runs over, the one named last changes fastest.
Arguments:
- pulses: bfloat16 [2, 512, 256, 4096], P(None, None, 'dop', 'rng'), may hold values from -60 to 60
- guard: int32 [4096], P('rng'), may hold values 0 or 1
- steer_index: int32 [256], P('dop'), may hold values from 0 to 63
Outputs:
- beams: float32 [256, 2, 4096], P('dop', None, 'rng')
The draws below stay inside these ranges and needn't reach their ends.
All inputs are finite; a program needn't handle non-finite values. No bound on the sum of `guard` on one device may be relied on, other than what follows from the above.
Results may differ from the reference program's by a relative error of at most 0.003.
The reference program's roundings to bfloat16 on the way count: a program that leaves them out, or rounds other values in their place, can miss the bound.
Values may be sent and summed in bfloat16 or wider, within the bound.
No kernel may reach another device: no remote copies, remote signals or barrier semaphores. Data moves between devices by JAX's collectives and lax.ppermute only.
A program may use at most 128 MiB of HBM per device.

```python
import math
import jax
import jax.numpy as jnp
from jax import lax

CH = 256
PULSES = 512
NANG = 64
BIN_DEV = 32
BINS = 256
CELLS = 4096
N_DOP = 8


def draw_pulses(key, part):
    key = jax.random.fold_in(key, 11)
    key_chan, key_base = jax.random.split(key, 2)
    shape = (2, PULSES, CH, CELLS)
    channel_amp = 10.0 ** (0.5 * jax.random.uniform(key_chan, (CH,), jnp.float32))
    cell_amp = 10.0 ** (0.5 * jnp.arange(CELLS, dtype=jnp.float32) / (CELLS - 1))
    amplitude = channel_amp[None, None, :, None] * cell_amp[None, None, None, :]
    values = amplitude * jnp.clip(jax.random.normal(key_base, shape, jnp.float32), -4.0, 4.0)
    return values.astype(jnp.bfloat16)


def place_ends(array, own_key, smallest, largest):
    longest = array.shape.index(max(array.shape))
    spots = []
    for shift in (0, 1):
        where = [jax.random.randint(jax.random.fold_in(own_key, axis), (), 0, length) for axis, length in enumerate(array.shape)]
        where[longest] = (where[longest] + shift) % array.shape[longest]
        spots.append(tuple(where))
    return array.at[spots[0]].set(smallest).at[spots[1]].set(largest)


def setup_inputs(seed: int = 0) -> dict:
    keys = jax.random.split(jax.random.key(seed), 4)
    pulses = draw_pulses(jax.random.fold_in(keys[3], 71), 0)
    guard = place_ends((jax.random.randint(keys[1], (CELLS,), 0, 4) < 1).astype(jnp.int32), jax.random.fold_in(keys[1], 1), 0, 1)
    steer_index = place_ends(jax.random.randint(keys[2], (BINS,), 0, NANG), jax.random.fold_in(keys[2], 1), 0, NANG - 1).astype(jnp.int32)
    return dict(pulses=pulses, guard=guard, steer_index=steer_index)


LOADING = 0.1

def doppler_table(period, bins):
    pulse_index = jnp.arange(period, dtype=jnp.int32)
    bin_index = jnp.arange(bins, dtype=jnp.int32)
    turn_count = pulse_index[:, None] * bin_index[None, :] % period
    phase_angle = 2.0 * math.pi / period * turn_count.astype(jnp.float32)
    window_taper = 0.54 - 0.46 * jnp.cos(2.0 * math.pi / (period - 1) * pulse_index.astype(jnp.float32))
    cosine = window_taper[:, None] * jnp.cos(phase_angle)
    sine_part = window_taper[:, None] * jnp.sin(phase_angle)
    return jnp.stack([jnp.stack([cosine, sine_part]), jnp.stack([-sine_part, cosine])]).astype(jnp.bfloat16)

def steering(indices, channels):
    sine_of = -0.9 + 1.8 * indices.astype(jnp.float32) / (NANG - 1)
    phase_angle = math.pi * jnp.arange(channels, dtype=jnp.float32)[None, :] * sine_of[:, None]
    return jnp.concatenate([jnp.cos(phase_angle), jnp.sin(phase_angle)], 1)

def covariance(snapshot, weight_rows):
    real_rows = snapshot[:, 0].astype(jnp.float32)
    imag_rows = snapshot[:, 1].astype(jnp.float32)
    stacked = jnp.concatenate([real_rows, imag_rows], 2)
    turned = jnp.concatenate([imag_rows, -real_rows], 2)
    masking = jnp.concatenate([weight_rows, weight_rows], 1).astype(jnp.float32)[:, None, :]
    left_side = jnp.stack([stacked * masking, turned * masking], 1)
    return jnp.einsum('bkir,bjr->bkij', left_side, stacked, precision=lax.Precision.HIGHEST)

def solve_weights(covariance_sum, steer_vectors, total_cells):
    channels = covariance_sum.shape[-1]
    real_block = covariance_sum[:, 0] / total_cells
    imag_block = covariance_sum[:, 1] / total_cells
    loading = LOADING * jnp.trace(real_block, axis1=1, axis2=2) / channels + 1e-05
    loaded = real_block + loading[:, None, None] * jnp.eye(channels, dtype=jnp.float32)
    full_matrix = jnp.concatenate([jnp.concatenate([loaded, -imag_block], 2), jnp.concatenate([imag_block, loaded], 2)], 1)
    lower = jnp.linalg.cholesky(full_matrix)
    first = lax.linalg.triangular_solve(lower, steer_vectors[:, :, None], left_side=True, lower=True)
    weights = lax.linalg.triangular_solve(lower, first, left_side=True, lower=True, transpose_a=True)[:, :, 0]
    return (weights.astype(jnp.bfloat16), loading)

def beamform(weights, snapshot):
    channels = snapshot.shape[2]
    real_w = weights[:, :channels]
    imag_w = weights[:, channels:]
    paired = jnp.stack([jnp.stack([real_w, imag_w], 1), jnp.stack([-imag_w, real_w], 1)], 1)
    return jnp.einsum('bokc,bkcr->bor', paired.astype(jnp.float32), snapshot.astype(jnp.float32), precision=lax.Precision.HIGHEST)

def reference(pulses, guard, steer_index):
    table = doppler_table(PULSES, BINS)
    flat = pulses.reshape(2 * PULSES, CH * CELLS)
    training = (1 - guard).astype(jnp.bfloat16)
    rows_mask = jnp.broadcast_to(training, (BIN_DEV, CELLS))

    def one_block(block):
        part_table = lax.dynamic_slice_in_dim(table, block * BIN_DEV, BIN_DEV, 3).reshape(2, 2 * PULSES, BIN_DEV)
        real_part = jnp.dot(part_table[0].T.astype(jnp.float32), flat.astype(jnp.float32), preferred_element_type=jnp.float32)
        imag_part = jnp.dot(part_table[1].T.astype(jnp.float32), flat.astype(jnp.float32), preferred_element_type=jnp.float32)
        snapshot = jnp.stack([real_part, imag_part], 1).reshape(BIN_DEV, 2, CH, CELLS).astype(jnp.bfloat16)
        covariance_sum = covariance(snapshot, rows_mask)
        steer_vectors = steering(lax.dynamic_slice_in_dim(steer_index, block * BIN_DEV, BIN_DEV), CH)
        weights, loading = solve_weights(covariance_sum, steer_vectors, CELLS)
        raw_beams = beamform(weights, snapshot)
        train_power = lax.optimization_barrier(jnp.sum(rows_mask.astype(jnp.float32)[:, None, :] * raw_beams * raw_beams, axis=(1, 2)))
        power = train_power / CELLS + loading * lax.optimization_barrier(jnp.sum(jnp.square(weights.astype(jnp.float32)), 1))
        return raw_beams * lax.rsqrt(power)[:, None, None]
    result = lax.map(one_block, jnp.arange(N_DOP, dtype=jnp.int32))
    return result.reshape(BINS, 2, CELLS)
```

```python
import functools, math
import jax, jax.numpy as jnp
from jax import lax
from jax.experimental import pallas as pl
from jax.experimental.pallas import tpu as pltpu
HI = lax.Precision.HIGHEST
CELLS=4096
NB=32

def lane(x, j):
    return jnp.broadcast_to(x[:, j:j+1], x.shape)
def sub(x, j):
    return jnp.broadcast_to(x[j:j+1, :], x.shape)

def gj1(ar, ai, n):
    row = lax.broadcasted_iota(jnp.int32, (8,128), 0)
    for j in range(n):
        g, jj = divmod(j, 8)
        rr, ri = sub(ar[g], jj), sub(ai[g], jj)
        t = 1.0 / lane(rr, j)
        nr, ni = rr * t, ri * t
        br, bi = [], []
        for h in range(n // 8):
            cr, ci = lane(ar[h], j), lane(ai[h], j)
            ur = ar[h] - (cr * nr - ci * ni)
            ui = ai[h] - (cr * ni + ci * nr)
            if h == g:
                ur = jnp.where(row == jj, nr, ur); ui = jnp.where(row == jj, ni, ui)
            br.append(ur); bi.append(ui)
        ar, ai = br, bi
    return ar, ai

def gj2(ar, ai, n):
    row = lax.broadcasted_iota(jnp.int32, (8,128), 0)
    for j in range(0, n, 2):
        g, jj = divmod(j, 8)
        pr, pi = sub(ar[g], jj), sub(ai[g], jj)
        qr, qi = sub(ar[g], jj+1), sub(ai[g], jj+1)
        a, d = lane(pr, j), lane(qr, j+1)
        b, e = lane(pr, j+1), lane(pi, j+1)
        t = 1.0 / (a * d - (b * b + e * e))
        npr = (d * pr - (b * qr - e * qi)) * t
        npi = (d * pi - (b * qi + e * qr)) * t
        nqr = (a * qr - (b * pr + e * pi)) * t
        nqi = (a * qi - (b * pi - e * pr)) * t
        br, bi = [], []
        for h in range(n // 8):
            cr, ci = lane(ar[h], j), lane(ai[h], j)
            dr, di = lane(ar[h], j+1), lane(ai[h], j+1)
            ur = ar[h] - ((cr * npr - ci * npi) + (dr * nqr - di * nqi))
            ui = ai[h] - ((cr * npi + ci * npr) + (dr * nqi + di * nqr))
            if h == g:
                ur = jnp.where(row == jj, npr, jnp.where(row == jj+1, nqr, ur))
                ui = jnp.where(row == jj, npi, jnp.where(row == jj+1, nqi, ui))
            br.append(ur); bi.append(ui)
        ar, ai = br, bi
    return ar, ai

def times_i(x, ch):
    tail = x[:, 2*ch:]
    lane_no = lax.broadcasted_iota(jnp.int32, tail.shape, 1)
    back, fwd = pltpu.roll(tail, 127, 1), pltpu.roll(tail, 1, 1)
    return jnp.concatenate([-x[:, ch:2*ch], x[:, :ch], jnp.where(lane_no == 0, -back, fwd)], 1)

def solve_in(w_ref, ch, gj, prec=HI):
    nb = NB
    n8 = nb // 8
    lanes = lax.broadcasted_iota(jnp.int32, (8,128), 1)
    rows = lax.broadcasted_iota(jnp.int32, (8,128), 0)
    def block(k, _):
        at = pl.ds(pl.multiple_of(k * nb, nb), nb)
        x = w_ref[at, :]
        ar, ai = [], []
        for h in range(n8):
            ar.append(jnp.where(lanes < nb, x[8*h:8*h+8, :128], jnp.where(lanes == nb + 8*h + rows, 1.0, 0.0)))
            ai.append(jnp.where(lanes < nb, x[8*h:8*h+8, ch:ch+128], 0.0))
        ar, ai = gj(ar, ai, nb)
        ar, ai = jnp.concatenate(ar, 0), jnp.concatenate(ai, 0)
        lhs = jnp.concatenate([ar[:, nb:2*nb], ai[:, nb:2*nb]], 1)
        y = jnp.dot(lhs, jnp.concatenate([x, times_i(x, ch)], 0), precision=prec, preferred_element_type=jnp.float32)
        yy = jnp.concatenate([y, times_i(y, ch)], 0)
        c = jnp.concatenate([w_ref[:, :nb], w_ref[:, ch:ch+nb]], 1)
        upd = w_ref[...] - jnp.dot(c, yy, precision=prec, preferred_element_type=jnp.float32)
        w_ref[...] = upd
        w_ref[at, :] = y
        w_ref[:, :ch] = pltpu.roll(w_ref[:, :ch], ch - nb, 1)
        w_ref[:, ch:2*ch] = pltpu.roll(w_ref[:, ch:2*ch], ch - nb, 1)
        return 0
    lax.fori_loop(0, ch // nb, block, 0)

def cov_kernel(x_ref, m_ref, rhs_ref, w_ref, ld_ref, acc_ref):
    ch = 256
    acc_ref[...] = jnp.zeros_like(acc_ref)
    def step(s, _):
        x = x_ref[:, pl.ds(s, 1)].reshape(8, 64, 128)
        m = jnp.broadcast_to(m_ref[pl.ds(s, 1), :].astype(jnp.bfloat16), (ch, 128))
        xr = x[:, :32].reshape(ch, 128) * m
        xi = x[:, 32:].reshape(ch, 128) * m
        a = jnp.concatenate([xr, xi], 1)
        b = jnp.concatenate([xi, -xr], 1)
        acc_ref[...] += lax.dot_general(jnp.concatenate([a, b], 0), a, (((1,), (1,)), ((), ())), preferred_element_type=jnp.float32)
        return 0
    lax.fori_loop(0, 32, step, 0)
    re = acc_ref[:ch] * (1.0 / CELLS)
    im = acc_ref[ch:] * (1.0 / CELLS)
    diag = lax.broadcasted_iota(jnp.int32, (ch, ch), 0) == lax.broadcasted_iota(jnp.int32, (ch, ch), 1)
    ld = 0.1 * jnp.sum(jnp.where(diag, re, 0.0), keepdims=True) / ch + 1e-5
    w_ref[:, :ch] = re + jnp.where(diag, ld, 0.0)
    w_ref[:, ch:2*ch] = im
    w_ref[:, 2*ch:] = rhs_ref[...]
    ld_ref[...] = jnp.broadcast_to(ld, ld_ref.shape)

def beam_part(x_ref, m_ref, w_ref, ld, out_ref):
    ch = 256
    wt = jnp.transpose(w_ref[:, 2*ch:])[:8]
    wt = wt.astype(jnp.bfloat16).astype(jnp.float32)
    wr, wi = wt[0:1], wt[1:2]
    first = lax.broadcasted_iota(jnp.int32, (8, ch), 0)
    lr = jnp.where(first == 0, wr, jnp.where(first == 1, -wi, 0.0)).astype(jnp.bfloat16)
    li = jnp.where(first == 0, wi, jnp.where(first == 1, wr, 0.0)).astype(jnp.bfloat16)
    lhs = jnp.concatenate([lr, li], 1)
    def step(s, p):
        x = x_ref[:, pl.ds(s, 1)].reshape(8, 64, 128)
        x2 = jnp.concatenate([x[:, :32].reshape(ch, 128), x[:, 32:].reshape(ch, 128)], 0)
        raw = jnp.dot(lhs, x2, preferred_element_type=jnp.float32)
        out_ref[pl.ds(s, 1)] = raw[:2].reshape(1, 2, 128)
        return p + raw * raw * m_ref[pl.ds(s, 1), :]
    p = lax.fori_loop(0, 32, step, jnp.zeros((8, 128), jnp.float32))
    sq = jnp.sum(jnp.where(first < 2, wt * wt, 0.0), keepdims=True)
    power = jnp.sum(p, keepdims=True) * (1.0 / CELLS) + ld * sq
    out_ref[...] = out_ref[...] * lax.rsqrt(power).reshape(1, 1, 1)

def full_kernel(gj, parts, x_ref, m_ref, rhs_ref, out_ref, w_ref, acc_ref, ld_ref):
    if "c" in parts: cov_kernel(x_ref, m_ref, rhs_ref, w_ref, ld_ref, acc_ref)
    else:
        w_ref[...] = jnp.zeros_like(w_ref)
        d = lax.broadcasted_iota(jnp.int32, (256, 256), 0) == lax.broadcasted_iota(jnp.int32, (256, 256), 1)
        w_ref[:, :256] = jnp.where(d, 2.0, 0.1)
        w_ref[:, 512:] = rhs_ref[...]
        ld_ref[...] = jnp.ones_like(ld_ref)
    if "s" in parts: solve_in(w_ref, 256, gj)
    if "b" in parts: beam_part(x_ref, m_ref, w_ref, ld_ref[:1, :1], out_ref)
    else: out_ref[...] = w_ref[:64, 512:].reshape(32, 2, 128)

def full(x, m, rhs, gj=gj1, parts="csb", interpret=False):
    return pl.pallas_call(
        functools.partial(full_kernel, gj, parts),
        out_shape=jax.ShapeDtypeStruct((32, 2, 128), jnp.float32),
        in_specs=[pl.BlockSpec(memory_space=pltpu.VMEM)] * 3,
        out_specs=pl.BlockSpec(memory_space=pltpu.VMEM),
        scratch_shapes=[pltpu.VMEM((256, 640), jnp.float32), pltpu.VMEM((512, 256), jnp.float32), pltpu.VMEM((8, 128), jnp.float32)],
        compiler_params=pltpu.CompilerParams(vmem_limit_bytes=40 * 2**20),
        name="solve", interpret=interpret,
    )(x, m, rhs)


from jax.sharding import PartitionSpec as P

NANG = 64


def doppler_table(period, bins):
    pulse_index = jnp.arange(period, dtype=jnp.int32)
    bin_index = jnp.arange(bins, dtype=jnp.int32)
    turn_count = pulse_index[:, None] * bin_index[None, :] % period
    phase_angle = 2.0 * math.pi / period * turn_count.astype(jnp.float32)
    window_taper = 0.54 - 0.46 * jnp.cos(
        2.0 * math.pi / (period - 1) * pulse_index.astype(jnp.float32)
    )
    cosine = window_taper[:, None] * jnp.cos(phase_angle)
    sine_part = window_taper[:, None] * jnp.sin(phase_angle)
    return jnp.stack([jnp.stack([cosine, sine_part]), jnp.stack([-sine_part, cosine])]).astype(
        jnp.bfloat16
    )


def steering(index, channels):
    sine_of = -0.9 + 1.8 * index.astype(jnp.float32) / (NANG - 1)
    phase_angle = math.pi * jnp.arange(channels, dtype=jnp.float32) * sine_of
    pair = jnp.stack([jnp.cos(phase_angle), jnp.sin(phase_angle)], 1)
    return jnp.pad(pair, ((0, 0), (0, 126)))


def on_device(pulses, guard, steer_index):
    bins = steer_index.shape[0] * lax.axis_size("dop")
    table = doppler_table(pulses.shape[1], bins)
    spectrum = jnp.einsum(
        "kjpb,jpcr->bkcr", table, pulses, preferred_element_type=jnp.float32
    ).astype(jnp.bfloat16)
    mask = 1.0 - lax.all_gather(guard, "rng", axis=0).astype(jnp.float32)
    rhs = steering(steer_index[lax.axis_index("rng")], 256)
    snapshot = lax.all_to_all(spectrum, ("dop", "rng"), split_axis=0, concat_axis=0, tiled=True)
    beams = full(snapshot.reshape(8, 32, 64, 128), mask, rhs, gj2)
    return lax.all_to_all(beams, "rng", split_axis=0, concat_axis=0, tiled=True)


def solution(mesh):
    return jax.shard_map(
        on_device,
        mesh=mesh,
        in_specs=(P(None, None, "dop", "rng"), P("rng"), P("dop")),
        out_specs=P("dop", None, "rng"),
        check_vma=False,
    )
```

```python
import functools
import math

import jax
import jax.numpy as jnp
from jax import lax
from jax.experimental import pallas as pl
from jax.experimental.pallas import tpu as pltpu

CELLS = 4096
CH = 256
NB = 32
LANES = 128


def dot(a, b):
    return jnp.dot(a, b, precision=lax.Precision.HIGHEST, preferred_element_type=jnp.float32)


def lane(x, j):
    return jnp.broadcast_to(x[:, j : j + 1], x.shape)


def sub(x, j):
    return jnp.broadcast_to(x[j : j + 1, :], x.shape)


def cmul(a, b):
    return a[0] * b[0] - a[1] * b[1], a[0] * b[1] + a[1] * b[0]


def cjmul(a, b):
    return a[0] * b[0] + a[1] * b[1], a[0] * b[1] - a[1] * b[0]


def add(a, b):
    return a[0] + b[0], a[1] + b[1]


def dif(a, b):
    return a[0] - b[0], a[1] - b[1]


def scale(s, a):
    return s * a[0], s * a[1]


def gauss_jordan(ar, ai, base):
    row = lax.broadcasted_iota(jnp.int32, (8, LANES), 0)
    for j in range(0, NB, 4):
        g, jj = divmod(j, 8)
        at = base + j
        p = [(sub(ar[g], jj + i), sub(ai[g], jj + i)) for i in range(4)]

        def entry(i, k):
            return lane(p[i][0], at + k), lane(p[i][1], at + k)

        d = [lane(p[k][0], at + k) for k in range(4)]
        a01, a02, a03 = entry(0, 1), entry(0, 2), entry(0, 3)
        a12, a13, a23 = entry(1, 2), entry(1, 3), entry(2, 3)
        t1 = 1.0 / (d[0] * d[1] - (a01[0] * a01[0] + a01[1] * a01[1]))
        w00 = scale(t1, dif(scale(d[1], a02), cmul(a01, a12)))
        w01 = scale(t1, dif(scale(d[1], a03), cmul(a01, a13)))
        w10 = scale(t1, dif(scale(d[0], a12), cjmul(a01, a02)))
        w11 = scale(t1, dif(scale(d[0], a13), cjmul(a01, a03)))
        s00 = d[2] - (cjmul(a02, w00)[0] + cjmul(a12, w10)[0])
        s11 = d[3] - (cjmul(a03, w01)[0] + cjmul(a13, w11)[0])
        s01 = dif(a23, add(cjmul(a02, w01), cjmul(a12, w11)))
        t2 = 1.0 / (s00 * s11 - (s01[0] * s01[0] + s01[1] * s01[1]))
        m0 = scale(t1, dif(scale(d[1], p[0]), cmul(a01, p[1])))
        m1 = scale(t1, dif(scale(d[0], p[1]), cjmul(a01, p[0])))
        q2 = dif(p[2], add(cjmul(a02, m0), cjmul(a12, m1)))
        q3 = dif(p[3], add(cjmul(a03, m0), cjmul(a13, m1)))
        n2 = scale(t2, dif(scale(s11, q2), cmul(s01, q3)))
        n3 = scale(t2, dif(scale(s00, q3), cjmul(s01, q2)))
        n0 = dif(m0, add(cmul(w00, n2), cmul(w01, n3)))
        n1 = dif(m1, add(cmul(w10, n2), cmul(w11, n3)))
        new = [n0, n1, n2, n3]
        br, bi = [], []
        for h in range(NB // 8):
            c = [(lane(ar[h], at + k), lane(ai[h], at + k)) for k in range(4)]
            u = add(add(cmul(c[0], n0), cmul(c[1], n1)), add(cmul(c[2], n2), cmul(c[3], n3)))
            ur, ui = ar[h] - u[0], ai[h] - u[1]
            if h == g:
                for i in range(4):
                    ur = jnp.where(row == jj + i, new[i][0], ur)
                    ui = jnp.where(row == jj + i, new[i][1], ui)
            br.append(ur)
            bi.append(ui)
        ar, ai = br, bi
    return ar, ai


def times_i(x, n):
    tail = x[:, 2 * n :]
    lane_no = lax.broadcasted_iota(jnp.int32, tail.shape, 1)
    back, fwd = pltpu.roll(tail, LANES - 1, 1), pltpu.roll(tail, 1, 1)
    return jnp.concatenate([-x[:, n : 2 * n], x[:, :n], jnp.where(lane_no == 0, -back, fwd)], 1)


def solve_in(w_ref):
    lanes = lax.broadcasted_iota(jnp.int32, (8, LANES), 1)
    rows = lax.broadcasted_iota(jnp.int32, (8, LANES), 0)
    dr, di = w_ref[:NB, :LANES], w_ref[:NB, CH : CH + LANES]
    for k in range(CH // NB):
        t, u = divmod(k, LANES // NB)
        base, other = NB * u, NB * ((u + 1) % (LANES // NB))
        inside = (lanes >= base) & (lanes < base + NB)
        ar, ai = [], []
        for h in range(NB // 8):
            unit = jnp.where(lanes == other + 8 * h + rows, 1.0, 0.0)
            ar.append(jnp.where(inside, dr[8 * h : 8 * h + 8], unit))
            ai.append(jnp.where(inside, di[8 * h : 8 * h + 8], 0.0))
        ar, ai = gauss_jordan(ar, ai, base)
        ar, ai = jnp.concatenate(ar, 0), jnp.concatenate(ai, 0)
        inv = jnp.concatenate([ar[:, other : other + NB], ai[:, other : other + NB]], 1)
        mine = slice(NB * k, NB * k + NB)
        live = slice(LANES * t, CH), slice(CH + LANES * t, 2 * CH), slice(2 * CH, 2 * CH + LANES)
        n = CH - LANES * t
        x = jnp.concatenate([w_ref[mine, s] for s in live], 1)
        y = dot(inv, jnp.concatenate([x, times_i(x, n)], 0))
        yy = jnp.concatenate([y, times_i(y, n)], 0)
        at = LANES * t + base
        c = jnp.concatenate([w_ref[:, at : at + NB], w_ref[:, CH + at : CH + at + NB]], 1)
        if k + 1 < CH // NB:
            nxt = slice(NB * k + NB, NB * k + 2 * NB)
            o = LANES * ((k + 1) // (LANES // NB) - t)
            e = LANES * t + o
            both = jnp.concatenate([yy[:, o : o + LANES], yy[:, n + o : n + o + LANES]], 1)
            step = dot(c[nxt], both)
            dr = w_ref[nxt, e : e + LANES] - step[:, :LANES]
            di = w_ref[nxt, CH + e : CH + e + LANES] - step[:, LANES:]
        upd = dot(c, yy)
        for s, o, m in zip(live, (0, n, 2 * n), (n, n, LANES)):
            w_ref[:, s] = w_ref[:, s] - upd[:, o : o + m]
            w_ref[mine, s] = y[:, o : o + m]


def cells_of(x_ref, s):
    x = x_ref[:, s]
    return x[:, :32].reshape(CH, LANES), x[:, 32:].reshape(CH, LANES)


UNROLL = 8


def cov_in(x_ref, m_ref, rhs_ref, w_ref, acc_ref):
    acc_ref[...] = jnp.zeros_like(acc_ref)

    def step(i, _):
        a, b = [], []
        for t in range(UNROLL):
            s = i * UNROLL + t
            xr, xi = cells_of(x_ref, s)
            m = jnp.broadcast_to(m_ref[pl.ds(s, 1), :].astype(jnp.bfloat16), (CH, LANES))
            xr, xi = xr * m, xi * m
            a += [xr, xi]
            b += [xi, -xr]
        a, b = jnp.concatenate(a, 1), jnp.concatenate(b, 1)
        acc_ref[...] += lax.dot_general(
            jnp.concatenate([a, b], 0), a, (((1,), (1,)), ((), ())), preferred_element_type=jnp.float32
        )
        return 0

    lax.fori_loop(0, CELLS // LANES // UNROLL, step, 0)
    re = acc_ref[:CH] * (1.0 / CELLS)
    im = acc_ref[CH:] * (1.0 / CELLS)
    diag = lax.broadcasted_iota(jnp.int32, (CH, CH), 0) == lax.broadcasted_iota(jnp.int32, (CH, CH), 1)
    loading = 0.1 * jnp.sum(jnp.where(diag, re, 0.0), keepdims=True) / CH + 1e-5
    w_ref[:, :CH] = re + jnp.where(diag, loading, 0.0)
    w_ref[:, CH : 2 * CH] = im
    w_ref[:, 2 * CH :] = rhs_ref[...]
    return loading


def beams_out(x_ref, m_ref, w_ref, loading, out_ref):
    wt = jnp.transpose(w_ref[:, 2 * CH :])[:8]
    wt = wt.astype(jnp.bfloat16).astype(jnp.float32)
    wr, wi = wt[0:1], wt[1:2]
    first = lax.broadcasted_iota(jnp.int32, (8, CH), 0)
    left = jnp.where(first == 0, wr, jnp.where(first == 1, -wi, 0.0))
    right = jnp.where(first == 0, wi, jnp.where(first == 1, wr, 0.0))
    lhs = jnp.concatenate([left, right], 1).astype(jnp.bfloat16)

    def step(i, p):
        x = []
        for t in range(UNROLL):
            x.append(jnp.concatenate(cells_of(x_ref, i * UNROLL + t), 0))
        raw = jnp.dot(lhs, jnp.concatenate(x, 1), preferred_element_type=jnp.float32)
        for t in range(UNROLL):
            s = i * UNROLL + t
            r = raw[:, LANES * t : LANES * t + LANES]
            out_ref[s] = r[:2]
            p = p + r * r * m_ref[pl.ds(s, 1), :]
        return p

    p = lax.fori_loop(0, CELLS // LANES // UNROLL, step, jnp.zeros((8, LANES), jnp.float32))
    sq = jnp.sum(jnp.where(first < 2, wt * wt, 0.0), keepdims=True)
    power = jnp.sum(p, keepdims=True) * (1.0 / CELLS) + loading * sq
    out_ref[...] = out_ref[...] * lax.rsqrt(power).reshape(1, 1, 1)


def bin_kernel(x_ref, m_ref, rhs_ref, out_ref, w_ref, acc_ref):
    loading = cov_in(x_ref, m_ref, rhs_ref, w_ref, acc_ref)
    solve_in(w_ref)
    beams_out(x_ref, m_ref, w_ref, loading, out_ref)


def one_bin(x, m, rhs):
    return pl.pallas_call(
        bin_kernel,
        out_shape=jax.ShapeDtypeStruct((CELLS // LANES, 2, LANES), jnp.float32),
        in_specs=[pl.BlockSpec(memory_space=pltpu.VMEM)] * 3,
        out_specs=pl.BlockSpec(memory_space=pltpu.VMEM),
        scratch_shapes=[
            pltpu.VMEM((CH, 2 * CH + LANES), jnp.float32),
            pltpu.VMEM((2 * CH, CH), jnp.float32),
        ],
        compiler_params=pltpu.CompilerParams(vmem_limit_bytes=40 * 2**20),
        name="one_bin",
    )(x, m, rhs)


from jax.sharding import PartitionSpec as P

NANG = 64


def doppler_table(period, bins):
    pulse_index = jnp.arange(period, dtype=jnp.int32)
    bin_index = jnp.arange(bins, dtype=jnp.int32)
    turn_count = pulse_index[:, None] * bin_index[None, :] % period
    phase_angle = 2.0 * math.pi / period * turn_count.astype(jnp.float32)
    window_taper = 0.54 - 0.46 * jnp.cos(
        2.0 * math.pi / (period - 1) * pulse_index.astype(jnp.float32)
    )
    cosine = window_taper[:, None] * jnp.cos(phase_angle)
    sine_part = window_taper[:, None] * jnp.sin(phase_angle)
    return jnp.stack([jnp.stack([cosine, sine_part]), jnp.stack([-sine_part, cosine])]).astype(
        jnp.bfloat16
    )


def steering(index, channels):
    sine_of = -0.9 + 1.8 * index.astype(jnp.float32) / (NANG - 1)
    phase_angle = math.pi * jnp.arange(channels, dtype=jnp.float32) * sine_of
    pair = jnp.stack([jnp.cos(phase_angle), jnp.sin(phase_angle)], 1)
    return jnp.pad(pair, ((0, 0), (0, LANES - 2)))


def on_device(pulses, guard, steer_index):
    bins = steer_index.shape[0] * lax.axis_size("dop")
    table = doppler_table(pulses.shape[1], bins)
    spectrum = jnp.einsum(
        "kjpb,jpcr->bkcr", table, pulses, preferred_element_type=jnp.float32
    ).astype(jnp.bfloat16)
    mask = 1.0 - lax.all_gather(guard, "rng", axis=0).astype(jnp.float32)
    rhs = steering(steer_index[lax.axis_index("rng")], CH)
    whole = lax.all_to_all(spectrum, ("dop", "rng"), split_axis=0, concat_axis=0, tiled=True)
    beams = one_bin(whole.reshape(8, CELLS // LANES, 64, LANES), mask, rhs)
    return lax.all_to_all(beams, "rng", split_axis=0, concat_axis=0, tiled=True)


def solution(mesh):
    return jax.shard_map(
        on_device,
        mesh=mesh,
        in_specs=(P(None, None, "dop", "rng"), P("rng"), P("dop")),
        out_specs=P("dop", None, "rng"),
        check_vma=False,
    )
```

```python
import functools
import math

import jax
import jax.numpy as jnp
import ml_dtypes
import numpy as np
from jax import lax
from jax.experimental import pallas as pl
from jax.experimental.pallas import tpu as pltpu

CELLS = 4096
CH = 256
NB = 32
LANES = 128
HBM = pltpu.MemorySpace.HBM
VMEM_LIMIT = 60 * 2**20
SLOTS = 10


def dot(a, b):
    return jnp.dot(a, b, precision=lax.Precision.HIGHEST, preferred_element_type=jnp.float32)


def lane(x, j):
    return jnp.broadcast_to(x[:, j : j + 1], x.shape)


def sub(x, j):
    return jnp.broadcast_to(x[j : j + 1, :], x.shape)


def cmul(a, b):
    return a[0] * b[0] - a[1] * b[1], a[0] * b[1] + a[1] * b[0]


def cjmul(a, b):
    return a[0] * b[0] + a[1] * b[1], a[0] * b[1] - a[1] * b[0]


def add(a, b):
    return a[0] + b[0], a[1] + b[1]


def dif(a, b):
    return a[0] - b[0], a[1] - b[1]


def scale(s, a):
    return s * a[0], s * a[1]


def gauss_jordan(ar, ai, base, s_ref):
    row = lax.broadcasted_iota(jnp.int32, (8, LANES), 0)
    for j in range(0, NB, 4):
        g, jj = divmod(j, 8)
        at = base + j
        slot = SLOTS * ((j // 4) % 2)

        def spread(k, i):
            return jnp.broadcast_to(s_ref[slot + k, i : i + 1, :], (8, LANES))

        col = [(lane(ar[g], at + k), lane(ai[g], at + k)) for k in range(4)]
        s_ref[slot] = ar[g]
        s_ref[slot + 1] = ai[g]
        for k in range(4):
            s_ref[slot + 2 + 2 * k] = col[k][0]
            s_ref[slot + 3 + 2 * k] = col[k][1]
        p = [(spread(0, jj + i), spread(1, jj + i)) for i in range(4)]

        def entry(i, k):
            return spread(2 + 2 * k, jj + i), spread(3 + 2 * k, jj + i)

        d = [spread(2 + 2 * k, jj + k) for k in range(4)]
        a01, a02, a03 = entry(0, 1), entry(0, 2), entry(0, 3)
        a12, a13, a23 = entry(1, 2), entry(1, 3), entry(2, 3)
        t1 = 1.0 / (d[0] * d[1] - (a01[0] * a01[0] + a01[1] * a01[1]))
        w00 = scale(t1, dif(scale(d[1], a02), cmul(a01, a12)))
        w01 = scale(t1, dif(scale(d[1], a03), cmul(a01, a13)))
        w10 = scale(t1, dif(scale(d[0], a12), cjmul(a01, a02)))
        w11 = scale(t1, dif(scale(d[0], a13), cjmul(a01, a03)))
        s00 = d[2] - (cjmul(a02, w00)[0] + cjmul(a12, w10)[0])
        s11 = d[3] - (cjmul(a03, w01)[0] + cjmul(a13, w11)[0])
        s01 = dif(a23, add(cjmul(a02, w01), cjmul(a12, w11)))
        t2 = 1.0 / (s00 * s11 - (s01[0] * s01[0] + s01[1] * s01[1]))
        m0 = scale(t1, dif(scale(d[1], p[0]), cmul(a01, p[1])))
        m1 = scale(t1, dif(scale(d[0], p[1]), cjmul(a01, p[0])))
        q2 = dif(p[2], add(cjmul(a02, m0), cjmul(a12, m1)))
        q3 = dif(p[3], add(cjmul(a03, m0), cjmul(a13, m1)))
        n2 = scale(t2, dif(scale(s11, q2), cmul(s01, q3)))
        n3 = scale(t2, dif(scale(s00, q3), cjmul(s01, q2)))
        n0 = dif(m0, add(cmul(w00, n2), cmul(w01, n3)))
        n1 = dif(m1, add(cmul(w10, n2), cmul(w11, n3)))
        new = [n0, n1, n2, n3]
        br, bi = [], []
        for h in range(NB // 8):
            c = col if h == g else [(lane(ar[h], at + k), lane(ai[h], at + k)) for k in range(4)]
            u = add(add(cmul(c[0], n0), cmul(c[1], n1)), add(cmul(c[2], n2), cmul(c[3], n3)))
            ur, ui = ar[h] - u[0], ai[h] - u[1]
            if h == g:
                for i in range(4):
                    ur = jnp.where(row == jj + i, new[i][0], ur)
                    ui = jnp.where(row == jj + i, new[i][1], ui)
            br.append(ur)
            bi.append(ui)
        ar, ai = br, bi
    return ar, ai


def times_i(x, n):
    tail = x[:, 2 * n :]
    lane_no = lax.broadcasted_iota(jnp.int32, tail.shape, 1)
    back, fwd = pltpu.roll(tail, LANES - 1, 1), pltpu.roll(tail, 1, 1)
    return jnp.concatenate([-x[:, n : 2 * n], x[:, :n], jnp.where(lane_no == 0, -back, fwd)], 1)


def solve_in(w_ref, s_ref):
    lanes = lax.broadcasted_iota(jnp.int32, (8, LANES), 1)
    rows = lax.broadcasted_iota(jnp.int32, (8, LANES), 0)
    dr, di = w_ref[:NB, :LANES], w_ref[:NB, CH : CH + LANES]
    for k in range(CH // NB):
        t, u = divmod(k, LANES // NB)
        base, other = NB * u, NB * ((u + 1) % (LANES // NB))
        inside = (lanes >= base) & (lanes < base + NB)
        ar, ai = [], []
        for h in range(NB // 8):
            unit = jnp.where(lanes == other + 8 * h + rows, 1.0, 0.0)
            ar.append(jnp.where(inside, dr[8 * h : 8 * h + 8], unit))
            ai.append(jnp.where(inside, di[8 * h : 8 * h + 8], 0.0))
        ar, ai = gauss_jordan(ar, ai, base, s_ref)
        ar, ai = jnp.concatenate(ar, 0), jnp.concatenate(ai, 0)
        inv = jnp.concatenate([ar[:, other : other + NB], ai[:, other : other + NB]], 1)
        mine = slice(NB * k, NB * k + NB)
        live = slice(LANES * t, CH), slice(CH + LANES * t, 2 * CH), slice(2 * CH, 2 * CH + LANES)
        n = CH - LANES * t
        x = jnp.concatenate([w_ref[mine, s] for s in live], 1)
        y = dot(inv, jnp.concatenate([x, times_i(x, n)], 0))
        yy = jnp.concatenate([y, times_i(y, n)], 0)
        at = LANES * t + base
        c = jnp.concatenate([w_ref[:, at : at + NB], w_ref[:, CH + at : CH + at + NB]], 1)
        if k + 1 < CH // NB:
            nxt = slice(NB * k + NB, NB * k + 2 * NB)
            o = LANES * ((k + 1) // (LANES // NB) - t)
            e = LANES * t + o
            both = jnp.concatenate([yy[:, o : o + LANES], yy[:, n + o : n + o + LANES]], 1)
            step = dot(c[nxt], both)
            dr = w_ref[nxt, e : e + LANES] - step[:, :LANES]
            di = w_ref[nxt, CH + e : CH + e + LANES] - step[:, LANES:]
        upd = dot(c, yy)
        for s, o, m in zip(live, (0, n, 2 * n), (n, n, LANES)):
            w_ref[:, s] = w_ref[:, s] - upd[:, o : o + m]
            w_ref[mine, s] = y[:, o : o + m]


def cells_of(x_ref, s):
    x = x_ref[s]
    return x[:, :32].reshape(CH, LANES), x[:, 32:].reshape(CH, LANES)


UNROLL = 8


def cov_in(x_ref, m_ref, rhs_ref, w_ref, acc_ref, arrive):
    acc_ref[...] = jnp.zeros_like(acc_ref)

    def step(i, _):
        arrive(i)
        a, b = [], []
        for t in range(UNROLL):
            s = i * UNROLL + t
            xr, xi = cells_of(x_ref, s)
            m = jnp.broadcast_to(m_ref[pl.ds(s, 1), :].astype(jnp.bfloat16), (CH, LANES))
            xr, xi = xr * m, xi * m
            a += [xr, xi]
            b += [xi, -xr]
        a, b = jnp.concatenate(a, 1), jnp.concatenate(b, 1)
        acc_ref[...] += lax.dot_general(
            jnp.concatenate([a, b], 0), a, (((1,), (1,)), ((), ())), preferred_element_type=jnp.float32
        )
        return 0

    lax.fori_loop(0, CELLS // LANES // UNROLL, step, 0)
    re = acc_ref[:CH] * (1.0 / CELLS)
    im = acc_ref[CH:] * (1.0 / CELLS)
    diag = lax.broadcasted_iota(jnp.int32, (CH, CH), 0) == lax.broadcasted_iota(jnp.int32, (CH, CH), 1)
    loading = 0.1 * jnp.sum(jnp.where(diag, re, 0.0), keepdims=True) / CH + 1e-5
    w_ref[:, :CH] = re + jnp.where(diag, loading, 0.0)
    w_ref[:, CH : 2 * CH] = im
    w_ref[:, 2 * CH :] = rhs_ref[...]
    return loading


def beams_out(x_ref, m_ref, w_ref, loading, out_ref):
    wt = jnp.transpose(w_ref[:, 2 * CH :])[:8]
    wt = wt.astype(jnp.bfloat16).astype(jnp.float32)
    wr, wi = wt[0:1], wt[1:2]
    first = lax.broadcasted_iota(jnp.int32, (8, CH), 0)
    left = jnp.where(first == 0, wr, jnp.where(first == 1, -wi, 0.0))
    right = jnp.where(first == 0, wi, jnp.where(first == 1, wr, 0.0))
    lhs = jnp.concatenate([left, right], 1).astype(jnp.bfloat16)

    def step(i, p):
        x = []
        for t in range(UNROLL):
            x.append(jnp.concatenate(cells_of(x_ref, i * UNROLL + t), 0))
        raw = jnp.dot(lhs, jnp.concatenate(x, 1), preferred_element_type=jnp.float32)
        for t in range(UNROLL):
            s = i * UNROLL + t
            r = raw[:, LANES * t : LANES * t + LANES]
            out_ref[s] = r[:2]
            p = p + r * r * m_ref[pl.ds(s, 1), :]
        return p

    p = lax.fori_loop(0, CELLS // LANES // UNROLL, step, jnp.zeros((8, LANES), jnp.float32))
    sq = jnp.sum(jnp.where(first < 2, wt * wt, 0.0), keepdims=True)
    power = jnp.sum(p, keepdims=True) * (1.0 / CELLS) + loading * sq
    out_ref[...] = out_ref[...] * lax.rsqrt(power).reshape(1, 1, 1)


def bin_kernel(x_hbm, m_ref, rhs_ref, out_ref, x_ref, w_ref, acc_ref, s_ref, in_sem):
    def fetch(i):
        rows = pl.ds(i * UNROLL, UNROLL)
        return pltpu.make_async_copy(x_hbm.at[rows], x_ref.at[rows], in_sem.at[i])

    for i in range(CELLS // LANES // UNROLL):
        fetch(i).start()
    loading = cov_in(x_ref, m_ref, rhs_ref, w_ref, acc_ref, lambda i: fetch(i).wait())
    solve_in(w_ref, s_ref)
    beams_out(x_ref, m_ref, w_ref, loading, out_ref)


def one_bin(x, m, rhs):
    return pl.pallas_call(
        bin_kernel,
        out_shape=jax.ShapeDtypeStruct((CELLS // LANES, 2, LANES), jnp.float32),
        in_specs=[pl.BlockSpec(memory_space=HBM)] + [pl.BlockSpec(memory_space=pltpu.VMEM)] * 2,
        out_specs=pl.BlockSpec(memory_space=pltpu.VMEM),
        scratch_shapes=[
            pltpu.VMEM(x.shape, x.dtype),
            pltpu.VMEM((CH, 2 * CH + LANES), jnp.float32),
            pltpu.VMEM((2 * CH, CH), jnp.float32),
            pltpu.VMEM((2 * SLOTS, 8, LANES), jnp.float32),
            pltpu.SemaphoreType.DMA((CELLS // LANES // UNROLL,)),
        ],
        compiler_params=pltpu.CompilerParams(vmem_limit_bytes=VMEM_LIMIT),
        name="one_bin",
    )(x, m, rhs)


GROUP = 16
IN_STRIDE = 24
OUT_STRIDE = 40


def doppler_rows(period, bins, blocks):
    pulse_index = np.arange(period, dtype=np.int32)
    bin_index = np.arange(bins, dtype=np.int32).reshape(blocks, -1).T.reshape(-1)
    turn_count = bin_index[:, None] * pulse_index[None, :] % period
    phase_angle = np.float32(2.0 * math.pi / period) * turn_count.astype(np.float32)
    window_taper = np.float32(0.54) - np.float32(0.46) * np.cos(
        np.float32(2.0 * math.pi / (period - 1)) * pulse_index.astype(np.float32)
    )
    cosine = window_taper * np.cos(phase_angle)
    sine_part = window_taper * np.sin(phase_angle)
    return np.concatenate(
        [np.concatenate([cosine, sine_part], 1), np.concatenate([-sine_part, cosine], 1)], 0
    ).astype(ml_dtypes.bfloat16)


PIECES = 4


def transform_kernel(
    table_hbm, x_hbm, out_hbm, table_ref, raw_ref, wide_ref, back_ref, out_ref, table_sem, in_sem, out_sem
):
    parts, pulses, channels = x_hbm.shape[:3]
    depth, bins, groups = parts * pulses, out_hbm.shape[0], channels // GROUP
    step = depth // PIECES

    def fetch(g, i):
        k, first = divmod(i * step, pulses)
        return pltpu.make_async_copy(
            x_hbm.at[k, pl.ds(first, step), pl.ds(GROUP * g, GROUP), :],
            raw_ref.at[g, pl.ds(step * i, step)],
            in_sem.at[g, i],
        )

    def send(g, k):
        return pltpu.make_async_copy(
            out_ref.at[g, k], out_hbm.at[:, k, pl.ds(GROUP * g, GROUP), :], out_sem.at[g, k]
        )

    table_copy = pltpu.make_async_copy(table_hbm, table_ref, table_sem)
    for g in range(groups):
        for i in range(PIECES):
            fetch(g, i).start()
        if g == 0:
            table_copy.start()
    flat = wide_ref.reshape(depth * IN_STRIDE, LANES)
    bflat = back_ref.reshape(bins * OUT_STRIDE, LANES)
    for g in range(groups):
        for i in range(PIECES):
            fetch(g, i).wait()
            rows = pl.ds(step * i, step)
            wide_ref[rows, :GROUP] = raw_ref[g, rows].astype(jnp.float32)
        if g == 0:
            table_copy.wait()
        for c in range(0, GROUP, 2):
            x = [flat[pl.ds(c + i, depth, stride=IN_STRIDE), :].astype(jnp.bfloat16) for i in range(2)]
            y = jnp.dot(table_ref[...], jnp.concatenate(x, 1), preferred_element_type=jnp.float32)
            for k in range(2):
                for i in range(2):
                    bflat[pl.ds(k * GROUP + c + i, bins, stride=OUT_STRIDE), :] = y[
                        bins * k : bins * k + bins, LANES * i : LANES * i + LANES
                    ]
        for k in range(2):
            out_ref[g, k] = back_ref[:, k * GROUP : k * GROUP + GROUP].astype(jnp.bfloat16)
            send(g, k).start()
    for g in range(groups):
        for k in range(2):
            send(g, k).wait()


def transform(pulses, bins, blocks):
    parts, period, channels, cells = pulses.shape
    table = jnp.asarray(doppler_rows(period, bins, blocks))
    groups, depth = channels // GROUP, parts * period
    return pl.pallas_call(
        transform_kernel,
        out_shape=jax.ShapeDtypeStruct((bins, 2, channels, cells), jnp.bfloat16),
        in_specs=[pl.BlockSpec(memory_space=HBM)] * 2,
        out_specs=pl.BlockSpec(memory_space=HBM),
        scratch_shapes=[
            pltpu.VMEM((2 * bins, depth), jnp.bfloat16),
            pltpu.VMEM((groups, depth, GROUP, cells), jnp.bfloat16),
            pltpu.VMEM((depth, IN_STRIDE, cells), jnp.float32),
            pltpu.VMEM((bins, OUT_STRIDE, cells), jnp.float32),
            pltpu.VMEM((groups, 2, bins, GROUP, cells), jnp.bfloat16),
            pltpu.SemaphoreType.DMA,
            pltpu.SemaphoreType.DMA((groups, PIECES)),
            pltpu.SemaphoreType.DMA((groups, 2)),
        ],
        compiler_params=pltpu.CompilerParams(vmem_limit_bytes=VMEM_LIMIT),
        name="transform",
    )(table, pulses)


from jax.sharding import PartitionSpec as P

NANG = 64


def steering(index, channels):
    sine_of = -0.9 + 1.8 * index.astype(jnp.float32) / (NANG - 1)
    phase_angle = math.pi * jnp.arange(channels, dtype=jnp.float32) * sine_of
    pair = jnp.stack([jnp.cos(phase_angle), jnp.sin(phase_angle)], 1)
    return jnp.pad(pair, ((0, 0), (0, LANES - 2)))


def on_device(pulses, guard, steer_index):
    bins = steer_index.shape[0] * lax.axis_size("dop")
    spectrum = transform(pulses, bins, lax.axis_size("dop"))
    mask = 1.0 - lax.all_gather(guard, "rng", axis=0).astype(jnp.float32)
    rhs = steering(steer_index[lax.axis_index("rng")], CH)
    whole = lax.all_to_all(spectrum, ("rng", "dop"), split_axis=0, concat_axis=0, tiled=True)
    beams = one_bin(whole.reshape(CELLS // LANES, 8, 64, LANES), mask, rhs)
    return lax.all_to_all(beams, "rng", split_axis=0, concat_axis=0, tiled=True)


def solution(mesh):
    return jax.shard_map(
        on_device,
        mesh=mesh,
        in_specs=(P(None, None, "dop", "rng"), P("rng"), P("dop")),
        out_specs=P("dop", None, "rng"),
        check_vma=False,
    )
```

```python
import functools
import math

import jax
import jax.numpy as jnp
import ml_dtypes
import numpy as np
from jax import lax
from jax.experimental import pallas as pl
from jax.experimental.pallas import tpu as pltpu

CELLS = 4096
CH = 256
NB = 32
LANES = 128
HBM = pltpu.MemorySpace.HBM
VMEM_LIMIT = 60 * 2**20
SLOTS = 14
PART = CH + LANES


def dot(a, b):
    return jnp.dot(a, b, precision=lax.Precision.HIGHEST, preferred_element_type=jnp.float32)


def lane(x, j):
    return jnp.broadcast_to(x[:, j : j + 1], x.shape)


def sub(x, j):
    return jnp.broadcast_to(x[j : j + 1, :], x.shape)


def cmul(a, b):
    return a[0] * b[0] - a[1] * b[1], a[0] * b[1] + a[1] * b[0]


def cjmul(a, b):
    return a[0] * b[0] + a[1] * b[1], a[0] * b[1] - a[1] * b[0]


def add(a, b):
    return a[0] + b[0], a[1] + b[1]


def dif(a, b):
    return a[0] - b[0], a[1] - b[1]


def scale(s, a):
    return s * a[0], s * a[1]


def gauss_jordan(tiles, base, s_ref):
    row = lax.broadcasted_iota(jnp.int32, (8, LANES), 0)
    for j in range(0, NB, 4):
        g, jj = divmod(j, 8)
        at = base + j
        slot = SLOTS * ((j // 4) % 2)

        def spread(k, i):
            return jnp.broadcast_to(s_ref[slot + k, i : i + 1, :], (8, LANES))

        def column(h):
            return [(lane(tiles[0][h][0], at + k), lane(tiles[0][h][1], at + k)) for k in range(4)]

        col = column(g)
        for k in range(4):
            s_ref[slot + 2 * k] = col[k][0]
            s_ref[slot + 2 * k + 1] = col[k][1]
        for n, tile in enumerate(tiles):
            s_ref[slot + 8 + 2 * n] = tile[g][0]
            s_ref[slot + 9 + 2 * n] = tile[g][1]

        def entry(i, k):
            return spread(2 * k, jj + i), spread(2 * k + 1, jj + i)

        d = [spread(2 * k, jj + k) for k in range(4)]
        a01, a02, a03 = entry(0, 1), entry(0, 2), entry(0, 3)
        a12, a13, a23 = entry(1, 2), entry(1, 3), entry(2, 3)
        t1 = 1.0 / (d[0] * d[1] - (a01[0] * a01[0] + a01[1] * a01[1]))
        w00 = scale(t1, dif(scale(d[1], a02), cmul(a01, a12)))
        w01 = scale(t1, dif(scale(d[1], a03), cmul(a01, a13)))
        w10 = scale(t1, dif(scale(d[0], a12), cjmul(a01, a02)))
        w11 = scale(t1, dif(scale(d[0], a13), cjmul(a01, a03)))
        s00 = d[2] - (cjmul(a02, w00)[0] + cjmul(a12, w10)[0])
        s11 = d[3] - (cjmul(a03, w01)[0] + cjmul(a13, w11)[0])
        s01 = dif(a23, add(cjmul(a02, w01), cjmul(a12, w11)))
        t2 = 1.0 / (s00 * s11 - (s01[0] * s01[0] + s01[1] * s01[1]))
        news = []
        for n in range(len(tiles)):
            p = [(spread(8 + 2 * n, jj + i), spread(9 + 2 * n, jj + i)) for i in range(4)]
            m0 = scale(t1, dif(scale(d[1], p[0]), cmul(a01, p[1])))
            m1 = scale(t1, dif(scale(d[0], p[1]), cjmul(a01, p[0])))
            q2 = dif(p[2], add(cjmul(a02, m0), cjmul(a12, m1)))
            q3 = dif(p[3], add(cjmul(a03, m0), cjmul(a13, m1)))
            n2 = scale(t2, dif(scale(s11, q2), cmul(s01, q3)))
            n3 = scale(t2, dif(scale(s00, q3), cjmul(s01, q2)))
            n0 = dif(m0, add(cmul(w00, n2), cmul(w01, n3)))
            n1 = dif(m1, add(cmul(w10, n2), cmul(w11, n3)))
            news.append([n0, n1, n2, n3])
        after = [[] for _ in tiles]
        for h in range(NB // 8):
            c = col if h == g else column(h)
            for n, tile in enumerate(tiles):
                new = news[n]
                u = add(
                    add(cmul(c[0], new[0]), cmul(c[1], new[1])), add(cmul(c[2], new[2]), cmul(c[3], new[3]))
                )
                ur, ui = dif(tile[h], u)
                if h == g:
                    for i in range(4):
                        ur = jnp.where(row == jj + i, new[i][0], ur)
                        ui = jnp.where(row == jj + i, new[i][1], ui)
                after[n].append((ur, ui))
        tiles = after
    return [[jnp.concatenate([piece[part] for piece in tile], 0) for part in range(2)] for tile in tiles]


def turned(re, im):
    return jnp.concatenate([jnp.concatenate([re, im], 1), jnp.concatenate([-im, re], 1)], 0)


def solve_in(w_ref, s_ref):
    parts = [(w_ref[:NB, o : o + LANES], w_ref[:NB, PART + o : PART + o + LANES]) for o in range(0, PART, LANES)]
    per_tile = LANES // NB
    for k in range(CH // NB):
        t, u = divmod(k, per_tile)
        mine, nxt = slice(NB * k, NB * k + NB), slice(NB * k + NB, NB * k + 2 * NB)
        tiles = [[(a[8 * h : 8 * h + 8], b[8 * h : 8 * h + 8]) for h in range(NB // 8)] for a, b in parts]
        tiles = gauss_jordan(tiles, NB * u, s_ref)
        re, im = (jnp.concatenate([tile[part] for tile in tiles], 1) for part in range(2))
        both = turned(re, im)
        n = PART - LANES * t
        at = LANES * t + NB * u
        c = jnp.concatenate([w_ref[:, at : at + NB], w_ref[:, PART + at : PART + at + NB]], 1)
        if k + 1 < CH // NB:
            step = dot(c[nxt], both)
            first = LANES * ((k + 1) // per_tile)
            parts = [
                (
                    w_ref[nxt, o : o + LANES] - step[:, o - LANES * t : o - LANES * t + LANES],
                    w_ref[nxt, PART + o : PART + o + LANES] - step[:, n + o - LANES * t : n + o - LANES * t + LANES],
                )
                for o in range(first, PART, LANES)
            ]
        upd = dot(c, both)
        for s, o, y in ((slice(LANES * t, PART), 0, re), (slice(PART + LANES * t, 2 * PART), n, im)):
            w_ref[:, s] = w_ref[:, s] - upd[:, o : o + n]
            w_ref[mine, s] = y


def cells_of(x_ref, s):
    x = x_ref[s]
    return x[:, :32].reshape(CH, LANES), x[:, 32:].reshape(CH, LANES)


UNROLL = 8


def cov_in(x_ref, m_ref, rhs_ref, w_ref, acc_ref, arrive):
    acc_ref[...] = jnp.zeros_like(acc_ref)

    def step(i, _):
        arrive(i)
        a, b = [], []
        for t in range(UNROLL):
            s = i * UNROLL + t
            xr, xi = cells_of(x_ref, s)
            m = jnp.broadcast_to(m_ref[pl.ds(s, 1), :].astype(jnp.bfloat16), (CH, LANES))
            xr, xi = xr * m, xi * m
            a += [xr, xi]
            b += [xi, -xr]
        a, b = jnp.concatenate(a, 1), jnp.concatenate(b, 1)
        acc_ref[...] += lax.dot_general(
            jnp.concatenate([a, b], 0), a, (((1,), (1,)), ((), ())), preferred_element_type=jnp.float32
        )
        return 0

    lax.fori_loop(0, CELLS // LANES // UNROLL, step, 0)
    re = acc_ref[:CH] * (1.0 / CELLS)
    im = acc_ref[CH:] * (1.0 / CELLS)
    diag = lax.broadcasted_iota(jnp.int32, (CH, CH), 0) == lax.broadcasted_iota(jnp.int32, (CH, CH), 1)
    loading = 0.1 * jnp.sum(jnp.where(diag, re, 0.0), keepdims=True) / CH + 1e-5
    w_ref[:, :CH] = re + jnp.where(diag, loading, 0.0)
    w_ref[:, CH:PART] = rhs_ref[0]
    w_ref[:, PART : PART + CH] = im
    w_ref[:, PART + CH :] = rhs_ref[1]
    return loading


def beams_out(x_ref, m_ref, w_ref, loading, out_ref):
    wr, wi = (
        jnp.transpose(w_ref[:, o : o + LANES])[:1].astype(jnp.bfloat16).astype(jnp.float32) for o in (CH, PART + CH)
    )
    first = lax.broadcasted_iota(jnp.int32, (8, CH), 0)
    left = jnp.where(first == 0, wr, jnp.where(first == 1, -wi, 0.0))
    right = jnp.where(first == 0, wi, jnp.where(first == 1, wr, 0.0))
    lhs = jnp.concatenate([left, right], 1).astype(jnp.bfloat16)

    def step(i, p):
        x = []
        for t in range(UNROLL):
            x.append(jnp.concatenate(cells_of(x_ref, i * UNROLL + t), 0))
        raw = jnp.dot(lhs, jnp.concatenate(x, 1), preferred_element_type=jnp.float32)
        for t in range(UNROLL):
            s = i * UNROLL + t
            r = raw[:, LANES * t : LANES * t + LANES]
            out_ref[s] = r[:2]
            p = p + r * r * m_ref[pl.ds(s, 1), :]
        return p

    p = lax.fori_loop(0, CELLS // LANES // UNROLL, step, jnp.zeros((8, LANES), jnp.float32))
    sq = jnp.sum(wr * wr + wi * wi, keepdims=True)
    power = jnp.sum(p, keepdims=True) * (1.0 / CELLS) + loading * sq
    out_ref[...] = out_ref[...] * lax.rsqrt(power).reshape(1, 1, 1)


def bin_kernel(x_hbm, m_ref, rhs_ref, out_ref, x_ref, w_ref, acc_ref, s_ref, in_sem):
    def fetch(i):
        rows = pl.ds(i * UNROLL, UNROLL)
        return pltpu.make_async_copy(x_hbm.at[rows], x_ref.at[rows], in_sem.at[i])

    for i in range(CELLS // LANES // UNROLL):
        fetch(i).start()
    loading = cov_in(x_ref, m_ref, rhs_ref, w_ref, acc_ref, lambda i: fetch(i).wait())
    solve_in(w_ref, s_ref)
    beams_out(x_ref, m_ref, w_ref, loading, out_ref)


def one_bin(x, m, rhs):
    return pl.pallas_call(
        bin_kernel,
        out_shape=jax.ShapeDtypeStruct((CELLS // LANES, 2, LANES), jnp.float32),
        in_specs=[pl.BlockSpec(memory_space=HBM)] + [pl.BlockSpec(memory_space=pltpu.VMEM)] * 2,
        out_specs=pl.BlockSpec(memory_space=pltpu.VMEM),
        scratch_shapes=[
            pltpu.VMEM(x.shape, x.dtype),
            pltpu.VMEM((CH, 2 * PART), jnp.float32),
            pltpu.VMEM((2 * CH, CH), jnp.float32),
            pltpu.VMEM((2 * SLOTS, 8, LANES), jnp.float32),
            pltpu.SemaphoreType.DMA((CELLS // LANES // UNROLL,)),
        ],
        compiler_params=pltpu.CompilerParams(vmem_limit_bytes=VMEM_LIMIT),
        name="one_bin",
    )(x, m, rhs)


GROUP = 16
IN_STRIDE = 24
OUT_STRIDE = 40


def doppler_rows(period, bins, blocks):
    pulse_index = np.arange(period, dtype=np.int32)
    bin_index = np.arange(bins, dtype=np.int32).reshape(blocks, -1).T.reshape(-1)
    turn_count = bin_index[:, None] * pulse_index[None, :] % period
    phase_angle = np.float32(2.0 * math.pi / period) * turn_count.astype(np.float32)
    window_taper = np.float32(0.54) - np.float32(0.46) * np.cos(
        np.float32(2.0 * math.pi / (period - 1)) * pulse_index.astype(np.float32)
    )
    cosine = window_taper * np.cos(phase_angle)
    sine_part = window_taper * np.sin(phase_angle)
    return np.concatenate(
        [np.concatenate([cosine, sine_part], 1), np.concatenate([-sine_part, cosine], 1)], 0
    ).astype(ml_dtypes.bfloat16)


PIECES = 2


def transform_kernel(
    table_hbm, x_hbm, out_hbm, table_ref, raw_ref, wide_ref, back_ref, out_ref, table_sem, in_sem, out_sem
):
    parts, pulses, channels = x_hbm.shape[:3]
    depth, bins, groups = parts * pulses, out_hbm.shape[0], channels // GROUP
    step = depth // PIECES

    def fetch(g, i):
        k, first = divmod(i * step, pulses)
        return pltpu.make_async_copy(
            x_hbm.at[k, pl.ds(first, step), pl.ds(GROUP * g, GROUP), :],
            raw_ref.at[g, pl.ds(step * i, step)],
            in_sem.at[g, i],
        )

    def send(g, k):
        return pltpu.make_async_copy(
            out_ref.at[g, k], out_hbm.at[:, k, pl.ds(GROUP * g, GROUP), :], out_sem.at[g, k]
        )

    table_copy = pltpu.make_async_copy(table_hbm, table_ref, table_sem)
    for i in range(PIECES):
        fetch(0, i).start()
    table_copy.start()
    flat = wide_ref.reshape(depth * IN_STRIDE, LANES)
    bflat = back_ref.reshape(bins * OUT_STRIDE, LANES)
    for g in range(groups):
        for i in range(PIECES):
            fetch(g, i).wait()
            if g + 1 < groups:
                fetch(g + 1, i).start()
            rows = pl.ds(step * i, step)
            wide_ref[rows, :GROUP] = raw_ref[g, rows].astype(jnp.float32)
        if g == 0:
            table_copy.wait()
        for c in range(0, GROUP, 2):
            x = [flat[pl.ds(c + i, depth, stride=IN_STRIDE), :].astype(jnp.bfloat16) for i in range(2)]
            y = jnp.dot(table_ref[...], jnp.concatenate(x, 1), preferred_element_type=jnp.float32)
            for k in range(2):
                for i in range(2):
                    bflat[pl.ds(k * GROUP + c + i, bins, stride=OUT_STRIDE), :] = y[
                        bins * k : bins * k + bins, LANES * i : LANES * i + LANES
                    ]
        for k in range(2):
            out_ref[g, k] = back_ref[:, k * GROUP : k * GROUP + GROUP].astype(jnp.bfloat16)
            send(g, k).start()
    for g in range(groups):
        for k in range(2):
            send(g, k).wait()


def transform(pulses, bins, blocks):
    parts, period, channels, cells = pulses.shape
    table = jnp.asarray(doppler_rows(period, bins, blocks))
    groups, depth = channels // GROUP, parts * period
    return pl.pallas_call(
        transform_kernel,
        out_shape=jax.ShapeDtypeStruct((bins, 2, channels, cells), jnp.bfloat16),
        in_specs=[pl.BlockSpec(memory_space=HBM)] * 2,
        out_specs=pl.BlockSpec(memory_space=HBM),
        scratch_shapes=[
            pltpu.VMEM((2 * bins, depth), jnp.bfloat16),
            pltpu.VMEM((groups, depth, GROUP, cells), jnp.bfloat16),
            pltpu.VMEM((depth, IN_STRIDE, cells), jnp.float32),
            pltpu.VMEM((bins, OUT_STRIDE, cells), jnp.float32),
            pltpu.VMEM((groups, 2, bins, GROUP, cells), jnp.bfloat16),
            pltpu.SemaphoreType.DMA,
            pltpu.SemaphoreType.DMA((groups, PIECES)),
            pltpu.SemaphoreType.DMA((groups, 2)),
        ],
        compiler_params=pltpu.CompilerParams(vmem_limit_bytes=VMEM_LIMIT),
        name="transform",
    )(table, pulses)


from jax.sharding import PartitionSpec as P

NANG = 64


def steering(index, channels):
    sine_of = -0.9 + 1.8 * index.astype(jnp.float32) / (NANG - 1)
    phase_angle = math.pi * jnp.arange(channels, dtype=jnp.float32) * sine_of
    pair = jnp.stack([jnp.cos(phase_angle), jnp.sin(phase_angle)])
    return jnp.pad(pair[:, :, None], ((0, 0), (0, 0), (0, LANES - 1)))


def on_device(pulses, guard, steer_index):
    bins = steer_index.shape[0] * lax.axis_size("dop")
    spectrum = transform(pulses, bins, lax.axis_size("dop"))
    mask = 1.0 - lax.all_gather(guard, "rng", axis=0).astype(jnp.float32)
    rhs = steering(steer_index[lax.axis_index("rng")], CH)
    whole = lax.all_to_all(spectrum, ("rng", "dop"), split_axis=0, concat_axis=0, tiled=True)
    beams = one_bin(whole.reshape(CELLS // LANES, 8, 64, LANES), mask, rhs)
    return lax.all_to_all(beams, "rng", split_axis=0, concat_axis=0, tiled=True)


def solution(mesh):
    return jax.shard_map(
        on_device,
        mesh=mesh,
        in_specs=(P(None, None, "dop", "rng"), P("rng"), P("dop")),
        out_specs=P("dop", None, "rng"),
        check_vma=False,
    )
```

```python
import functools
import math

import jax
import jax.numpy as jnp
import ml_dtypes
import numpy as np
from jax import lax
from jax.experimental import pallas as pl
from jax.experimental.pallas import tpu as pltpu

CELLS = 4096
CH = 256
NB = 32
LANES = 128
HBM = pltpu.MemorySpace.HBM
VMEM_LIMIT = 60 * 2**20
SLOTS = 14
PART = CH + LANES


def dot(a, b):
    return jnp.dot(a, b, precision=lax.Precision.HIGHEST, preferred_element_type=jnp.float32)


def lane(x, j):
    return jnp.broadcast_to(x[:, j : j + 1], x.shape)


def sub(x, j):
    return jnp.broadcast_to(x[j : j + 1, :], x.shape)


def cmul(a, b):
    return a[0] * b[0] - a[1] * b[1], a[0] * b[1] + a[1] * b[0]


def cjmul(a, b):
    return a[0] * b[0] + a[1] * b[1], a[0] * b[1] - a[1] * b[0]


def add(a, b):
    return a[0] + b[0], a[1] + b[1]


def dif(a, b):
    return a[0] - b[0], a[1] - b[1]


def scale(s, a):
    return s * a[0], s * a[1]


def gauss_jordan(tiles, base, s_ref):
    row = lax.broadcasted_iota(jnp.int32, (8, LANES), 0)
    for j in range(0, NB, 4):
        g, jj = divmod(j, 8)
        at = base + j
        slot = SLOTS * ((j // 4) % 2)

        def spread(k, i):
            return jnp.broadcast_to(s_ref[slot + k, i : i + 1, :], (8, LANES))

        def column(h):
            return [(lane(tiles[0][h][0], at + k), lane(tiles[0][h][1], at + k)) for k in range(4)]

        col = column(g)
        for k in range(4):
            s_ref[slot + 2 * k] = col[k][0]
            s_ref[slot + 2 * k + 1] = col[k][1]
        for n, tile in enumerate(tiles):
            s_ref[slot + 8 + 2 * n] = tile[g][0]
            s_ref[slot + 9 + 2 * n] = tile[g][1]

        def entry(i, k):
            return spread(2 * k, jj + i), spread(2 * k + 1, jj + i)

        d = [spread(2 * k, jj + k) for k in range(4)]
        a01, a02, a03 = entry(0, 1), entry(0, 2), entry(0, 3)
        a12, a13, a23 = entry(1, 2), entry(1, 3), entry(2, 3)
        t1 = 1.0 / (d[0] * d[1] - (a01[0] * a01[0] + a01[1] * a01[1]))
        w00 = scale(t1, dif(scale(d[1], a02), cmul(a01, a12)))
        w01 = scale(t1, dif(scale(d[1], a03), cmul(a01, a13)))
        w10 = scale(t1, dif(scale(d[0], a12), cjmul(a01, a02)))
        w11 = scale(t1, dif(scale(d[0], a13), cjmul(a01, a03)))
        s00 = d[2] - (cjmul(a02, w00)[0] + cjmul(a12, w10)[0])
        s11 = d[3] - (cjmul(a03, w01)[0] + cjmul(a13, w11)[0])
        s01 = dif(a23, add(cjmul(a02, w01), cjmul(a12, w11)))
        t2 = 1.0 / (s00 * s11 - (s01[0] * s01[0] + s01[1] * s01[1]))
        news = []
        for n in range(len(tiles)):
            p = [(spread(8 + 2 * n, jj + i), spread(9 + 2 * n, jj + i)) for i in range(4)]
            m0 = scale(t1, dif(scale(d[1], p[0]), cmul(a01, p[1])))
            m1 = scale(t1, dif(scale(d[0], p[1]), cjmul(a01, p[0])))
            q2 = dif(p[2], add(cjmul(a02, m0), cjmul(a12, m1)))
            q3 = dif(p[3], add(cjmul(a03, m0), cjmul(a13, m1)))
            n2 = scale(t2, dif(scale(s11, q2), cmul(s01, q3)))
            n3 = scale(t2, dif(scale(s00, q3), cjmul(s01, q2)))
            n0 = dif(m0, add(cmul(w00, n2), cmul(w01, n3)))
            n1 = dif(m1, add(cmul(w10, n2), cmul(w11, n3)))
            news.append([n0, n1, n2, n3])
        after = [[] for _ in tiles]
        for h in range(NB // 8):
            c = col if h == g else column(h)
            for n, tile in enumerate(tiles):
                new = news[n]
                u = add(
                    add(cmul(c[0], new[0]), cmul(c[1], new[1])), add(cmul(c[2], new[2]), cmul(c[3], new[3]))
                )
                ur, ui = dif(tile[h], u)
                if h == g:
                    for i in range(4):
                        ur = jnp.where(row == jj + i, new[i][0], ur)
                        ui = jnp.where(row == jj + i, new[i][1], ui)
                after[n].append((ur, ui))
        tiles = after
    return [[jnp.concatenate([piece[part] for piece in tile], 0) for part in range(2)] for tile in tiles]


def turned(re, im):
    return jnp.concatenate([jnp.concatenate([re, im], 1), jnp.concatenate([-im, re], 1)], 0)


def live_tiles(k):
    per_tile = LANES // NB
    if k == 0:
        return [0, LANES, CH]
    if k < per_tile:
        return [0, LANES]
    return [LANES, 0] if k == per_tile else [LANES]


def solve_in(w_ref, s_ref):
    def block(rows, at):
        return w_ref[rows, at : at + LANES], w_ref[rows, PART + at : PART + at + LANES]

    parts = [block(slice(0, NB), at) for at in live_tiles(0)]
    for k in range(CH // NB):
        mine, nxt = slice(NB * k, NB * k + NB), slice(NB * k + NB, NB * k + 2 * NB)
        live, then = live_tiles(k), live_tiles(min(k + 1, CH // NB - 1))
        moved = (live[-1], then[0]) if len(then) < len(live) else None
        tiles = [[(a[8 * h : 8 * h + 8], b[8 * h : 8 * h + 8]) for h in range(NB // 8)] for a, b in parts]
        tiles = gauss_jordan(tiles, NB * k % LANES, s_ref)
        re, im = (jnp.concatenate([tile[part] for tile in tiles], 1) for part in range(2))
        both = turned(re, im)
        n = LANES * len(live)
        c = jnp.concatenate([w_ref[:, NB * k : NB * k + NB], w_ref[:, PART + NB * k : PART + NB * k + NB]], 1)
        if k + 1 < CH // NB:
            step = dot(c[nxt], both)
            fresh = {}
            for i, at in enumerate(live):
                a, b = block(nxt, at)
                o = LANES * i
                fresh[at] = a - step[:, o : o + LANES], b - step[:, n + o : n + o + LANES]
            if moved:
                lane0 = lax.broadcasted_iota(jnp.int32, (NB, LANES), 1) == 0
                fresh[moved[1]] = tuple(jnp.where(lane0, a, b) for a, b in zip(fresh[moved[0]], fresh[moved[1]]))
            parts = [fresh[at] for at in then]
        upd = dot(c, both)
        for i, at in enumerate(live):
            for first, o, y in ((at, LANES * i, re), (PART + at, n + LANES * i, im)):
                s = slice(first, first + LANES)
                w_ref[:, s] = w_ref[:, s] - upd[:, o : o + LANES]
                w_ref[mine, s] = y[:, LANES * i : LANES * i + LANES]
        if moved:
            lane0 = lax.broadcasted_iota(jnp.int32, (CH, LANES), 1) == 0
            for first in (0, PART):
                s, d = (slice(first + at, first + at + LANES) for at in moved)
                w_ref[:, d] = jnp.where(lane0, w_ref[:, s], w_ref[:, d])


def cells_of(x_ref, s):
    x = x_ref[s]
    return x[:, :32].reshape(CH, LANES), x[:, 32:].reshape(CH, LANES)


UNROLL = 8


def cov_in(x_ref, m_ref, rhs_ref, w_ref, acc_ref, arrive):
    acc_ref[...] = jnp.zeros_like(acc_ref)

    def step(i, _):
        arrive(i)
        a, b = [], []
        for t in range(UNROLL):
            s = i * UNROLL + t
            xr, xi = cells_of(x_ref, s)
            m = jnp.broadcast_to(m_ref[pl.ds(s, 1), :].astype(jnp.bfloat16), (CH, LANES))
            xr, xi = xr * m, xi * m
            a += [xr, xi]
            b += [xi, -xr]
        a, b = jnp.concatenate(a, 1), jnp.concatenate(b, 1)
        acc_ref[...] += lax.dot_general(
            jnp.concatenate([a, b], 0), a, (((1,), (1,)), ((), ())), preferred_element_type=jnp.float32
        )
        return 0

    lax.fori_loop(0, CELLS // LANES // UNROLL, step, 0)
    re = acc_ref[:CH] * (1.0 / CELLS)
    im = acc_ref[CH:] * (1.0 / CELLS)
    diag = lax.broadcasted_iota(jnp.int32, (CH, CH), 0) == lax.broadcasted_iota(jnp.int32, (CH, CH), 1)
    loading = 0.1 * jnp.sum(jnp.where(diag, re, 0.0), keepdims=True) / CH + 1e-5
    w_ref[:, :CH] = re + jnp.where(diag, loading, 0.0)
    w_ref[:, CH:PART] = rhs_ref[0]
    w_ref[:, PART : PART + CH] = im
    w_ref[:, PART + CH :] = rhs_ref[1]
    return loading


def beams_out(x_ref, m_ref, w_ref, loading, out_ref):
    wr, wi = (
        jnp.transpose(w_ref[:, o : o + LANES])[:1].astype(jnp.bfloat16).astype(jnp.float32) for o in (LANES, PART + LANES)
    )
    first = lax.broadcasted_iota(jnp.int32, (8, CH), 0)
    left = jnp.where(first == 0, wr, jnp.where(first == 1, -wi, 0.0))
    right = jnp.where(first == 0, wi, jnp.where(first == 1, wr, 0.0))
    lhs = jnp.concatenate([left, right], 1).astype(jnp.bfloat16)

    def step(i, p):
        x = []
        for t in range(UNROLL):
            x.append(jnp.concatenate(cells_of(x_ref, i * UNROLL + t), 0))
        raw = jnp.dot(lhs, jnp.concatenate(x, 1), preferred_element_type=jnp.float32)
        for t in range(UNROLL):
            s = i * UNROLL + t
            r = raw[:, LANES * t : LANES * t + LANES]
            out_ref[s] = r[:2]
            p = p + r * r * m_ref[pl.ds(s, 1), :]
        return p

    p = lax.fori_loop(0, CELLS // LANES // UNROLL, step, jnp.zeros((8, LANES), jnp.float32))
    sq = jnp.sum(wr * wr + wi * wi, keepdims=True)
    power = jnp.sum(p, keepdims=True) * (1.0 / CELLS) + loading * sq
    out_ref[...] = out_ref[...] * lax.rsqrt(power).reshape(1, 1, 1)


def bin_kernel(x_hbm, m_ref, rhs_ref, out_ref, x_ref, w_ref, acc_ref, s_ref, in_sem):
    def fetch(i):
        rows = pl.ds(i * UNROLL, UNROLL)
        return pltpu.make_async_copy(x_hbm.at[rows], x_ref.at[rows], in_sem.at[i])

    for i in range(CELLS // LANES // UNROLL):
        fetch(i).start()
    loading = cov_in(x_ref, m_ref, rhs_ref, w_ref, acc_ref, lambda i: fetch(i).wait())
    solve_in(w_ref, s_ref)
    beams_out(x_ref, m_ref, w_ref, loading, out_ref)


def one_bin(x, m, rhs):
    return pl.pallas_call(
        bin_kernel,
        out_shape=jax.ShapeDtypeStruct((CELLS // LANES, 2, LANES), jnp.float32),
        in_specs=[pl.BlockSpec(memory_space=HBM)] + [pl.BlockSpec(memory_space=pltpu.VMEM)] * 2,
        out_specs=pl.BlockSpec(memory_space=pltpu.VMEM),
        scratch_shapes=[
            pltpu.VMEM(x.shape, x.dtype),
            pltpu.VMEM((CH, 2 * PART), jnp.float32),
            pltpu.VMEM((2 * CH, CH), jnp.float32),
            pltpu.VMEM((2 * SLOTS, 8, LANES), jnp.float32),
            pltpu.SemaphoreType.DMA((CELLS // LANES // UNROLL,)),
        ],
        compiler_params=pltpu.CompilerParams(vmem_limit_bytes=VMEM_LIMIT),
        name="one_bin",
    )(x, m, rhs)


GROUP = 16
IN_STRIDE = 24
OUT_STRIDE = 40


def doppler_rows(period, bins, blocks):
    pulse_index = np.arange(period, dtype=np.int32)
    bin_index = np.arange(bins, dtype=np.int32).reshape(blocks, -1).T.reshape(-1)
    turn_count = bin_index[:, None] * pulse_index[None, :] % period
    phase_angle = np.float32(2.0 * math.pi / period) * turn_count.astype(np.float32)
    window_taper = np.float32(0.54) - np.float32(0.46) * np.cos(
        np.float32(2.0 * math.pi / (period - 1)) * pulse_index.astype(np.float32)
    )
    cosine = window_taper * np.cos(phase_angle)
    sine_part = window_taper * np.sin(phase_angle)
    return np.concatenate(
        [np.concatenate([cosine, sine_part], 1), np.concatenate([-sine_part, cosine], 1)], 0
    ).astype(ml_dtypes.bfloat16)


PIECES = 2


def transform_kernel(
    table_hbm, x_hbm, out_hbm, table_ref, raw_ref, wide_ref, back_ref, out_ref, table_sem, in_sem, out_sem
):
    parts, pulses, channels = x_hbm.shape[:3]
    depth, bins, groups = parts * pulses, out_hbm.shape[0], channels // GROUP
    step = depth // PIECES

    def fetch(g, i):
        k, first = divmod(i * step, pulses)
        return pltpu.make_async_copy(
            x_hbm.at[k, pl.ds(first, step), pl.ds(GROUP * g, GROUP), :],
            raw_ref.at[g, pl.ds(step * i, step)],
            in_sem.at[g, i],
        )

    def send(g, k):
        return pltpu.make_async_copy(
            out_ref.at[g, k], out_hbm.at[:, k, pl.ds(GROUP * g, GROUP), :], out_sem.at[g, k]
        )

    table_copy = pltpu.make_async_copy(table_hbm, table_ref, table_sem)
    for i in range(PIECES):
        fetch(0, i).start()
    table_copy.start()
    flat = wide_ref.reshape(depth * IN_STRIDE, LANES)
    bflat = back_ref.reshape(bins * OUT_STRIDE, LANES)
    for g in range(groups):
        for i in range(PIECES):
            fetch(g, i).wait()
            if g + 1 < groups:
                fetch(g + 1, i).start()
            rows = pl.ds(step * i, step)
            wide_ref[rows, :GROUP] = raw_ref[g, rows].astype(jnp.float32)
        if g == 0:
            table_copy.wait()
        for c in range(0, GROUP, 2):
            x = [flat[pl.ds(c + i, depth, stride=IN_STRIDE), :].astype(jnp.bfloat16) for i in range(2)]
            y = jnp.dot(table_ref[...], jnp.concatenate(x, 1), preferred_element_type=jnp.float32)
            for k in range(2):
                for i in range(2):
                    bflat[pl.ds(k * GROUP + c + i, bins, stride=OUT_STRIDE), :] = y[
                        bins * k : bins * k + bins, LANES * i : LANES * i + LANES
                    ]
        for k in range(2):
            out_ref[g, k] = back_ref[:, k * GROUP : k * GROUP + GROUP].astype(jnp.bfloat16)
            send(g, k).start()
    for g in range(groups):
        for k in range(2):
            send(g, k).wait()


def transform(pulses, bins, blocks):
    parts, period, channels, cells = pulses.shape
    table = jnp.asarray(doppler_rows(period, bins, blocks))
    groups, depth = channels // GROUP, parts * period
    return pl.pallas_call(
        transform_kernel,
        out_shape=jax.ShapeDtypeStruct((bins, 2, channels, cells), jnp.bfloat16),
        in_specs=[pl.BlockSpec(memory_space=HBM)] * 2,
        out_specs=pl.BlockSpec(memory_space=HBM),
        scratch_shapes=[
            pltpu.VMEM((2 * bins, depth), jnp.bfloat16),
            pltpu.VMEM((groups, depth, GROUP, cells), jnp.bfloat16),
            pltpu.VMEM((depth, IN_STRIDE, cells), jnp.float32),
            pltpu.VMEM((bins, OUT_STRIDE, cells), jnp.float32),
            pltpu.VMEM((groups, 2, bins, GROUP, cells), jnp.bfloat16),
            pltpu.SemaphoreType.DMA,
            pltpu.SemaphoreType.DMA((groups, PIECES)),
            pltpu.SemaphoreType.DMA((groups, 2)),
        ],
        compiler_params=pltpu.CompilerParams(vmem_limit_bytes=VMEM_LIMIT),
        name="transform",
    )(table, pulses)


from jax.sharding import PartitionSpec as P

NANG = 64


def steering(index, channels):
    sine_of = -0.9 + 1.8 * index.astype(jnp.float32) / (NANG - 1)
    phase_angle = math.pi * jnp.arange(channels, dtype=jnp.float32) * sine_of
    pair = jnp.stack([jnp.cos(phase_angle), jnp.sin(phase_angle)])
    return jnp.pad(pair[:, :, None], ((0, 0), (0, 0), (0, LANES - 1)))


def on_device(pulses, guard, steer_index):
    bins = steer_index.shape[0] * lax.axis_size("dop")
    spectrum = transform(pulses, bins, lax.axis_size("dop"))
    mask = 1.0 - lax.all_gather(guard, "rng", axis=0).astype(jnp.float32)
    rhs = steering(steer_index[lax.axis_index("rng")], CH)
    whole = lax.all_to_all(spectrum, ("rng", "dop"), split_axis=0, concat_axis=0, tiled=True)
    beams = one_bin(whole.reshape(CELLS // LANES, 8, 64, LANES), mask, rhs)
    return lax.all_to_all(beams, "rng", split_axis=0, concat_axis=0, tiled=True)


def solution(mesh):
    return jax.shard_map(
        on_device,
        mesh=mesh,
        in_specs=(P(None, None, "dop", "rng"), P("rng"), P("dop")),
        out_specs=P("dop", None, "rng"),
        check_vma=False,
    )
```

```python
import functools
import math

import jax
import jax.numpy as jnp
import ml_dtypes
import numpy as np
from jax import lax
from jax.experimental import pallas as pl
from jax.experimental.pallas import tpu as pltpu

CELLS = 4096
CH = 256
NB = 32
LANES = 128
HBM = pltpu.MemorySpace.HBM
VMEM_LIMIT = 60 * 2**20
SLOTS = 14
PART = CH + LANES


def dot(a, b):
    return jnp.dot(a, b, precision=lax.Precision.HIGHEST, preferred_element_type=jnp.float32)


def lane(x, j):
    return jnp.broadcast_to(x[:, j : j + 1], x.shape)


def sub(x, j):
    return jnp.broadcast_to(x[j : j + 1, :], x.shape)


def cmul(a, b):
    return a[0] * b[0] - a[1] * b[1], a[0] * b[1] + a[1] * b[0]


def cjmul(a, b):
    return a[0] * b[0] + a[1] * b[1], a[0] * b[1] - a[1] * b[0]


def add(a, b):
    return a[0] + b[0], a[1] + b[1]


def dif(a, b):
    return a[0] - b[0], a[1] - b[1]


def scale(s, a):
    return s * a[0], s * a[1]


def gauss_jordan(tiles, base, s_ref):
    row = lax.broadcasted_iota(jnp.int32, (8, LANES), 0)
    for j in range(0, NB, 4):
        g, jj = divmod(j, 8)
        at = base + j
        slot = SLOTS * ((j // 4) % 2)

        def spread(k, i):
            return jnp.broadcast_to(s_ref[slot + k, i : i + 1, :], (8, LANES))

        def column(h):
            return [(lane(tiles[0][h][0], at + k), lane(tiles[0][h][1], at + k)) for k in range(4)]

        if jj == 0:
            col = column(g)
            ahead = [tuple(lane(piece, at + 4 + k) for piece in tiles[0][g]) for k in range(4)]
        else:
            col = ahead
        for k in range(4):
            s_ref[slot + 2 * k] = col[k][0]
            s_ref[slot + 2 * k + 1] = col[k][1]
        for n, tile in enumerate(tiles):
            s_ref[slot + 8 + 2 * n] = tile[g][0]
            s_ref[slot + 9 + 2 * n] = tile[g][1]

        def entry(i, k):
            return spread(2 * k, jj + i), spread(2 * k + 1, jj + i)

        d = [spread(2 * k, jj + k) for k in range(4)]
        a01, a02, a03 = entry(0, 1), entry(0, 2), entry(0, 3)
        a12, a13, a23 = entry(1, 2), entry(1, 3), entry(2, 3)
        t1 = 1.0 / (d[0] * d[1] - (a01[0] * a01[0] + a01[1] * a01[1]))
        w00 = scale(t1, dif(scale(d[1], a02), cmul(a01, a12)))
        w01 = scale(t1, dif(scale(d[1], a03), cmul(a01, a13)))
        w10 = scale(t1, dif(scale(d[0], a12), cjmul(a01, a02)))
        w11 = scale(t1, dif(scale(d[0], a13), cjmul(a01, a03)))
        s00 = d[2] - (cjmul(a02, w00)[0] + cjmul(a12, w10)[0])
        s11 = d[3] - (cjmul(a03, w01)[0] + cjmul(a13, w11)[0])
        s01 = dif(a23, add(cjmul(a02, w01), cjmul(a12, w11)))
        t2 = 1.0 / (s00 * s11 - (s01[0] * s01[0] + s01[1] * s01[1]))

        def new_rows(p):
            m0 = scale(t1, dif(scale(d[1], p[0]), cmul(a01, p[1])))
            m1 = scale(t1, dif(scale(d[0], p[1]), cjmul(a01, p[0])))
            q2 = dif(p[2], add(cjmul(a02, m0), cjmul(a12, m1)))
            q3 = dif(p[3], add(cjmul(a03, m0), cjmul(a13, m1)))
            n2 = scale(t2, dif(scale(s11, q2), cmul(s01, q3)))
            n3 = scale(t2, dif(scale(s00, q3), cjmul(s01, q2)))
            n0 = dif(m0, add(cmul(w00, n2), cmul(w01, n3)))
            n1 = dif(m1, add(cmul(w10, n2), cmul(w11, n3)))
            return [n0, n1, n2, n3]

        def less(piece, c, new):
            u = add(add(cmul(c[0], new[0]), cmul(c[1], new[1])), add(cmul(c[2], new[2]), cmul(c[3], new[3])))
            return dif(piece, u)

        def with_rows(piece, new):
            for i in range(4):
                piece = tuple(jnp.where(row == jj + i, new[i][part], piece[part]) for part in range(2))
            return piece

        if jj == 0:
            turned_rows = new_rows([(c[0], -c[1]) for c in col])
            for k in range(4):
                new = [(sub(v[0], 4 + k), sub(v[1], 4 + k)) for v in turned_rows]
                ahead[k] = with_rows(less(ahead[k], col, new), new)
        news = []
        for n in range(len(tiles)):
            news.append(new_rows([(spread(8 + 2 * n, jj + i), spread(9 + 2 * n, jj + i)) for i in range(4)]))
        after = [[] for _ in tiles]
        for h in range(NB // 8):
            c = col if h == g else column(h)
            for n, tile in enumerate(tiles):
                piece = less(tile[h], c, news[n])
                after[n].append(with_rows(piece, news[n]) if h == g else piece)
        tiles = after
    return [[jnp.concatenate([piece[part] for piece in tile], 0) for part in range(2)] for tile in tiles]


def turned(re, im):
    return jnp.concatenate([jnp.concatenate([re, im], 1), jnp.concatenate([-im, re], 1)], 0)


def live_tiles(k):
    per_tile = LANES // NB
    if k == 0:
        return [0, LANES, CH]
    if k < per_tile:
        return [0, LANES]
    return [LANES, 0] if k == per_tile else [LANES]


def solve_in(w_ref, s_ref):
    def block(rows, at):
        return w_ref[rows, at : at + LANES], w_ref[rows, PART + at : PART + at + LANES]

    parts = [block(slice(0, NB), at) for at in live_tiles(0)]
    for k in range(CH // NB):
        mine, nxt = slice(NB * k, NB * k + NB), slice(NB * k + NB, NB * k + 2 * NB)
        live, then = live_tiles(k), live_tiles(min(k + 1, CH // NB - 1))
        moved = (live[-1], then[0]) if len(then) < len(live) else None
        tiles = [[(a[8 * h : 8 * h + 8], b[8 * h : 8 * h + 8]) for h in range(NB // 8)] for a, b in parts]
        tiles = gauss_jordan(tiles, NB * k % LANES, s_ref)
        re, im = (jnp.concatenate([tile[part] for tile in tiles], 1) for part in range(2))
        both = turned(re, im)
        n = LANES * len(live)
        c = jnp.concatenate([w_ref[:, NB * k : NB * k + NB], w_ref[:, PART + NB * k : PART + NB * k + NB]], 1)
        if k + 1 < CH // NB:
            step = dot(c[nxt], both)
            fresh = {}
            for i, at in enumerate(live):
                a, b = block(nxt, at)
                o = LANES * i
                fresh[at] = a - step[:, o : o + LANES], b - step[:, n + o : n + o + LANES]
            if moved:
                lane0 = lax.broadcasted_iota(jnp.int32, (NB, LANES), 1) == 0
                fresh[moved[1]] = tuple(jnp.where(lane0, a, b) for a, b in zip(fresh[moved[0]], fresh[moved[1]]))
            parts = [fresh[at] for at in then]
        upd = dot(c, both)
        for i, at in enumerate(live):
            for first, o, y in ((at, LANES * i, re), (PART + at, n + LANES * i, im)):
                s = slice(first, first + LANES)
                w_ref[:, s] = w_ref[:, s] - upd[:, o : o + LANES]
                w_ref[mine, s] = y[:, LANES * i : LANES * i + LANES]
        if moved:
            lane0 = lax.broadcasted_iota(jnp.int32, (CH, LANES), 1) == 0
            for first in (0, PART):
                s, d = (slice(first + at, first + at + LANES) for at in moved)
                w_ref[:, d] = jnp.where(lane0, w_ref[:, s], w_ref[:, d])


def cells_of(x_ref, s):
    x = x_ref[s]
    return x[:, :32].reshape(CH, LANES), x[:, 32:].reshape(CH, LANES)


UNROLL = 16


def cov_in(x_ref, m_ref, rhs_ref, w_ref, acc_ref, arrive):
    acc_ref[...] = jnp.zeros_like(acc_ref)

    def step(i, _):
        arrive(i)
        a, b = [], []
        for t in range(UNROLL):
            s = i * UNROLL + t
            xr, xi = cells_of(x_ref, s)
            m = jnp.broadcast_to(m_ref[pl.ds(s, 1), :].astype(jnp.bfloat16), (CH, LANES))
            xr, xi = xr * m, xi * m
            a += [xr, xi]
            b += [xi, -xr]
        a, b = jnp.concatenate(a, 1), jnp.concatenate(b, 1)
        acc_ref[...] += lax.dot_general(
            jnp.concatenate([a, b], 0), a, (((1,), (1,)), ((), ())), preferred_element_type=jnp.float32
        )
        return 0

    lax.fori_loop(0, CELLS // LANES // UNROLL, step, 0)
    re = acc_ref[:CH] * (1.0 / CELLS)
    im = acc_ref[CH:] * (1.0 / CELLS)
    diag = lax.broadcasted_iota(jnp.int32, (CH, CH), 0) == lax.broadcasted_iota(jnp.int32, (CH, CH), 1)
    loading = 0.1 * jnp.sum(jnp.where(diag, re, 0.0), keepdims=True) / CH + 1e-5
    w_ref[:, :CH] = re + jnp.where(diag, loading, 0.0)
    w_ref[:, CH:PART] = rhs_ref[0]
    w_ref[:, PART : PART + CH] = im
    w_ref[:, PART + CH :] = rhs_ref[1]
    return loading


def beams_out(x_ref, m_ref, w_ref, loading, out_ref):
    wr, wi = (
        jnp.transpose(w_ref[:, o : o + LANES])[:1].astype(jnp.bfloat16).astype(jnp.float32) for o in (LANES, PART + LANES)
    )
    first = lax.broadcasted_iota(jnp.int32, (8, CH), 0)
    left = jnp.where(first == 0, wr, jnp.where(first == 1, -wi, 0.0))
    right = jnp.where(first == 0, wi, jnp.where(first == 1, wr, 0.0))
    lhs = jnp.concatenate([left, right], 1).astype(jnp.bfloat16)

    def step(i, p):
        x = []
        for t in range(UNROLL):
            x.append(jnp.concatenate(cells_of(x_ref, i * UNROLL + t), 0))
        raw = jnp.dot(lhs, jnp.concatenate(x, 1), preferred_element_type=jnp.float32)
        for t in range(UNROLL):
            s = i * UNROLL + t
            r = raw[:, LANES * t : LANES * t + LANES]
            out_ref[s] = r[:2]
            p = p + r * r * m_ref[pl.ds(s, 1), :]
        return p

    p = lax.fori_loop(0, CELLS // LANES // UNROLL, step, jnp.zeros((8, LANES), jnp.float32))
    sq = jnp.sum(wr * wr + wi * wi, keepdims=True)
    power = jnp.sum(p, keepdims=True) * (1.0 / CELLS) + loading * sq
    out_ref[...] = out_ref[...] * lax.rsqrt(power).reshape(1, 1, 1)


def bin_kernel(x_hbm, m_ref, rhs_ref, out_ref, x_ref, w_ref, acc_ref, s_ref, in_sem):
    def fetch(i):
        rows = pl.ds(i * UNROLL, UNROLL)
        return pltpu.make_async_copy(x_hbm.at[rows], x_ref.at[rows], in_sem.at[i])

    for i in range(CELLS // LANES // UNROLL):
        fetch(i).start()
    loading = cov_in(x_ref, m_ref, rhs_ref, w_ref, acc_ref, lambda i: fetch(i).wait())
    solve_in(w_ref, s_ref)
    beams_out(x_ref, m_ref, w_ref, loading, out_ref)


def one_bin(x, m, rhs):
    return pl.pallas_call(
        bin_kernel,
        out_shape=jax.ShapeDtypeStruct((CELLS // LANES, 2, LANES), jnp.float32),
        in_specs=[pl.BlockSpec(memory_space=HBM)] + [pl.BlockSpec(memory_space=pltpu.VMEM)] * 2,
        out_specs=pl.BlockSpec(memory_space=pltpu.VMEM),
        scratch_shapes=[
            pltpu.VMEM(x.shape, x.dtype),
            pltpu.VMEM((CH, 2 * PART), jnp.float32),
            pltpu.VMEM((2 * CH, CH), jnp.float32),
            pltpu.VMEM((2 * SLOTS, 8, LANES), jnp.float32),
            pltpu.SemaphoreType.DMA((CELLS // LANES // UNROLL,)),
        ],
        compiler_params=pltpu.CompilerParams(vmem_limit_bytes=VMEM_LIMIT),
        name="one_bin",
    )(x, m, rhs)


GROUP = 16
IN_STRIDE = 24
OUT_STRIDE = 40


def doppler_rows(period, bins, blocks):
    pulse_index = np.arange(period, dtype=np.int32)
    bin_index = np.arange(bins, dtype=np.int32).reshape(blocks, -1).T.reshape(-1)
    turn_count = bin_index[:, None] * pulse_index[None, :] % period
    phase_angle = np.float32(2.0 * math.pi / period) * turn_count.astype(np.float32)
    window_taper = np.float32(0.54) - np.float32(0.46) * np.cos(
        np.float32(2.0 * math.pi / (period - 1)) * pulse_index.astype(np.float32)
    )
    cosine = window_taper * np.cos(phase_angle)
    sine_part = window_taper * np.sin(phase_angle)
    return np.concatenate(
        [np.concatenate([cosine, sine_part], 1), np.concatenate([-sine_part, cosine], 1)], 0
    ).astype(ml_dtypes.bfloat16)


PIECES = 2


def transform_kernel(
    table_hbm, x_hbm, out_hbm, table_ref, raw_ref, wide_ref, back_ref, out_ref, table_sem, in_sem, out_sem
):
    parts, pulses, channels = x_hbm.shape[:3]
    depth, bins, groups = parts * pulses, out_hbm.shape[0], channels // GROUP
    step = depth // PIECES

    def fetch(g, i):
        k, first = divmod(i * step, pulses)
        return pltpu.make_async_copy(
            x_hbm.at[k, pl.ds(first, step), pl.ds(GROUP * g, GROUP), :],
            raw_ref.at[g, pl.ds(step * i, step)],
            in_sem.at[g, i],
        )

    def send(g, k):
        return pltpu.make_async_copy(
            out_ref.at[g, k], out_hbm.at[:, k, pl.ds(GROUP * g, GROUP), :], out_sem.at[g, k]
        )

    table_copy = pltpu.make_async_copy(table_hbm, table_ref, table_sem)
    for i in range(PIECES):
        fetch(0, i).start()
    table_copy.start()
    flat = wide_ref.reshape((depth + 1) * IN_STRIDE, LANES)
    bflat = back_ref.reshape((bins + 1) * OUT_STRIDE, LANES)
    for g in range(groups):
        for i in range(PIECES):
            fetch(g, i).wait()
            if g + 1 < groups:
                fetch(g + 1, i).start()
            rows = pl.ds(step * i, step)
            wide_ref[rows, :GROUP] = raw_ref[g, rows].astype(jnp.float32)
        if g == 0:
            table_copy.wait()
        for c in range(0, GROUP, 2):
            x = [flat[pl.ds(c + i, depth, stride=IN_STRIDE), :].astype(jnp.bfloat16) for i in range(2)]
            y = jnp.dot(table_ref[...], jnp.concatenate(x, 1), preferred_element_type=jnp.float32)
            for k in range(2):
                for i in range(2):
                    bflat[pl.ds(k * GROUP + c + i, bins, stride=OUT_STRIDE), :] = y[
                        bins * k : bins * k + bins, LANES * i : LANES * i + LANES
                    ]
        for k in range(2):
            out_ref[g, k] = back_ref[:bins, k * GROUP : k * GROUP + GROUP].astype(jnp.bfloat16)
            send(g, k).start()
    for g in range(groups):
        for k in range(2):
            send(g, k).wait()


def transform(pulses, bins, blocks):
    parts, period, channels, cells = pulses.shape
    table = jnp.asarray(doppler_rows(period, bins, blocks))
    groups, depth = channels // GROUP, parts * period
    return pl.pallas_call(
        transform_kernel,
        out_shape=jax.ShapeDtypeStruct((bins, 2, channels, cells), jnp.bfloat16),
        in_specs=[pl.BlockSpec(memory_space=HBM)] * 2,
        out_specs=pl.BlockSpec(memory_space=HBM),
        scratch_shapes=[
            pltpu.VMEM((2 * bins, depth), jnp.bfloat16),
            pltpu.VMEM((groups, depth, GROUP, cells), jnp.bfloat16),
            pltpu.VMEM((depth + 1, IN_STRIDE, cells), jnp.float32),
            pltpu.VMEM((bins + 1, OUT_STRIDE, cells), jnp.float32),
            pltpu.VMEM((groups, 2, bins, GROUP, cells), jnp.bfloat16),
            pltpu.SemaphoreType.DMA,
            pltpu.SemaphoreType.DMA((groups, PIECES)),
            pltpu.SemaphoreType.DMA((groups, 2)),
        ],
        compiler_params=pltpu.CompilerParams(vmem_limit_bytes=VMEM_LIMIT),
        name="transform",
    )(table, pulses)


from jax.sharding import PartitionSpec as P

NANG = 64


def steering(index, channels):
    sine_of = -0.9 + 1.8 * index.astype(jnp.float32) / (NANG - 1)
    phase_angle = math.pi * jnp.arange(channels, dtype=jnp.float32) * sine_of
    pair = jnp.stack([jnp.cos(phase_angle), jnp.sin(phase_angle)])
    return jnp.pad(pair[:, :, None], ((0, 0), (0, 0), (0, LANES - 1)))


def on_device(pulses, guard, steer_index):
    bins = steer_index.shape[0] * lax.axis_size("dop")
    spectrum = transform(pulses, bins, lax.axis_size("dop"))
    mask = 1.0 - lax.all_gather(guard, "rng", axis=0).astype(jnp.float32)
    rhs = steering(steer_index[lax.axis_index("rng")], CH)
    whole = lax.all_to_all(spectrum, ("rng", "dop"), split_axis=0, concat_axis=0, tiled=True)
    beams = one_bin(whole.reshape(CELLS // LANES, 8, 64, LANES), mask, rhs)
    return lax.all_to_all(beams, "rng", split_axis=0, concat_axis=0, tiled=True)


def solution(mesh):
    return jax.shard_map(
        on_device,
        mesh=mesh,
        in_specs=(P(None, None, "dop", "rng"), P("rng"), P("dop")),
        out_specs=P("dop", None, "rng"),
        check_vma=False,
    )
```

```python
import functools
import math

import jax
import jax.numpy as jnp
import ml_dtypes
import numpy as np
from jax import lax
from jax.experimental import pallas as pl
from jax.experimental.pallas import tpu as pltpu

CELLS = 4096
CH = 256
NB = 32
LANES = 128
HBM = pltpu.MemorySpace.HBM
VMEM_LIMIT = 60 * 2**20
SLOTS = 14
PART = CH + LANES


def dot(a, b):
    return jnp.dot(a, b, precision=lax.Precision.HIGHEST, preferred_element_type=jnp.float32)


def lane(x, j):
    return jnp.broadcast_to(x[:, j : j + 1], x.shape)


def sub(x, j):
    return jnp.broadcast_to(x[j : j + 1, :], x.shape)


def cmul(a, b):
    return a[0] * b[0] - a[1] * b[1], a[0] * b[1] + a[1] * b[0]


def cjmul(a, b):
    return a[0] * b[0] + a[1] * b[1], a[0] * b[1] - a[1] * b[0]


def add(a, b):
    return a[0] + b[0], a[1] + b[1]


def dif(a, b):
    return a[0] - b[0], a[1] - b[1]


def scale(s, a):
    return s * a[0], s * a[1]


def gauss_jordan(tiles, base, s_ref):
    row = lax.broadcasted_iota(jnp.int32, (8, LANES), 0)
    for j in range(0, NB, 4):
        g, jj = divmod(j, 8)
        at = base + j
        slot = SLOTS * ((j // 4) % 2)

        def spread(k, i):
            return jnp.broadcast_to(s_ref[slot + k, i : i + 1, :], (8, LANES))

        def column(h):
            return [(lane(tiles[0][h][0], at + k), lane(tiles[0][h][1], at + k)) for k in range(4)]

        if jj == 0:
            col = column(g)
            ahead = [tuple(lane(piece, at + 4 + k) for piece in tiles[0][g]) for k in range(4)]
        else:
            col = ahead
        for k in range(4):
            s_ref[slot + 2 * k] = col[k][0]
            s_ref[slot + 2 * k + 1] = col[k][1]
        for n, tile in enumerate(tiles):
            s_ref[slot + 8 + 2 * n] = tile[g][0]
            s_ref[slot + 9 + 2 * n] = tile[g][1]

        def entry(i, k):
            return spread(2 * k, jj + i), spread(2 * k + 1, jj + i)

        d = [spread(2 * k, jj + k) for k in range(4)]
        a01, a02, a03 = entry(0, 1), entry(0, 2), entry(0, 3)
        a12, a13, a23 = entry(1, 2), entry(1, 3), entry(2, 3)
        t1 = 1.0 / (d[0] * d[1] - (a01[0] * a01[0] + a01[1] * a01[1]))
        w00 = scale(t1, dif(scale(d[1], a02), cmul(a01, a12)))
        w01 = scale(t1, dif(scale(d[1], a03), cmul(a01, a13)))
        w10 = scale(t1, dif(scale(d[0], a12), cjmul(a01, a02)))
        w11 = scale(t1, dif(scale(d[0], a13), cjmul(a01, a03)))
        s00 = d[2] - (cjmul(a02, w00)[0] + cjmul(a12, w10)[0])
        s11 = d[3] - (cjmul(a03, w01)[0] + cjmul(a13, w11)[0])
        s01 = dif(a23, add(cjmul(a02, w01), cjmul(a12, w11)))
        t2 = 1.0 / (s00 * s11 - (s01[0] * s01[0] + s01[1] * s01[1]))

        def new_rows(p):
            m0 = scale(t1, dif(scale(d[1], p[0]), cmul(a01, p[1])))
            m1 = scale(t1, dif(scale(d[0], p[1]), cjmul(a01, p[0])))
            q2 = dif(p[2], add(cjmul(a02, m0), cjmul(a12, m1)))
            q3 = dif(p[3], add(cjmul(a03, m0), cjmul(a13, m1)))
            n2 = scale(t2, dif(scale(s11, q2), cmul(s01, q3)))
            n3 = scale(t2, dif(scale(s00, q3), cjmul(s01, q2)))
            n0 = dif(m0, add(cmul(w00, n2), cmul(w01, n3)))
            n1 = dif(m1, add(cmul(w10, n2), cmul(w11, n3)))
            return [n0, n1, n2, n3]

        def less(piece, c, new):
            u = add(add(cmul(c[0], new[0]), cmul(c[1], new[1])), add(cmul(c[2], new[2]), cmul(c[3], new[3])))
            return dif(piece, u)

        def with_rows(piece, new):
            for i in range(4):
                piece = tuple(jnp.where(row == jj + i, new[i][part], piece[part]) for part in range(2))
            return piece

        if jj == 0:
            turned_rows = new_rows([(c[0], -c[1]) for c in col])
            for k in range(4):
                new = [(sub(v[0], 4 + k), sub(v[1], 4 + k)) for v in turned_rows]
                ahead[k] = with_rows(less(ahead[k], col, new), new)
        news = []
        for n in range(len(tiles)):
            news.append(new_rows([(spread(8 + 2 * n, jj + i), spread(9 + 2 * n, jj + i)) for i in range(4)]))
        after = [[] for _ in tiles]
        for h in range(NB // 8):
            c = col if h == g else column(h)
            for n, tile in enumerate(tiles):
                piece = less(tile[h], c, news[n])
                after[n].append(with_rows(piece, news[n]) if h == g else piece)
        tiles = after
    return [[jnp.concatenate([piece[part] for piece in tile], 0) for part in range(2)] for tile in tiles]


def turned(re, im):
    return jnp.concatenate([jnp.concatenate([re, im], 1), jnp.concatenate([-im, re], 1)], 0)


def live_tiles(k):
    per_tile = LANES // NB
    if k == 0:
        return [0, LANES, CH]
    if k < per_tile:
        return [0, LANES]
    return [LANES, 0] if k == per_tile else [LANES]


def solve_in(w_ref, s_ref):
    def block(rows, at):
        return w_ref[rows, at : at + LANES], w_ref[rows, PART + at : PART + at + LANES]

    parts = [block(slice(0, NB), at) for at in live_tiles(0)]
    for k in range(CH // NB):
        mine, nxt = slice(NB * k, NB * k + NB), slice(NB * k + NB, NB * k + 2 * NB)
        live, then = live_tiles(k), live_tiles(min(k + 1, CH // NB - 1))
        moved = (live[-1], then[0]) if len(then) < len(live) else None
        tiles = [[(a[8 * h : 8 * h + 8], b[8 * h : 8 * h + 8]) for h in range(NB // 8)] for a, b in parts]
        tiles = gauss_jordan(tiles, NB * k % LANES, s_ref)
        re, im = (jnp.concatenate([tile[part] for tile in tiles], 1) for part in range(2))
        both = turned(re, im)
        n = LANES * len(live)
        c = jnp.concatenate([w_ref[:, NB * k : NB * k + NB], w_ref[:, PART + NB * k : PART + NB * k + NB]], 1)
        if k + 1 < CH // NB:
            step = dot(c[nxt], both)
            fresh = {}
            for i, at in enumerate(live):
                a, b = block(nxt, at)
                o = LANES * i
                fresh[at] = a - step[:, o : o + LANES], b - step[:, n + o : n + o + LANES]
            if moved:
                lane0 = lax.broadcasted_iota(jnp.int32, (NB, LANES), 1) == 0
                fresh[moved[1]] = tuple(jnp.where(lane0, a, b) for a, b in zip(fresh[moved[0]], fresh[moved[1]]))
            parts = [fresh[at] for at in then]
        upd = dot(c, both)
        for i, at in enumerate(live):
            for first, o, y in ((at, LANES * i, re), (PART + at, n + LANES * i, im)):
                s = slice(first, first + LANES)
                w_ref[:, s] = w_ref[:, s] - upd[:, o : o + LANES]
                w_ref[mine, s] = y[:, LANES * i : LANES * i + LANES]
        if moved:
            lane0 = lax.broadcasted_iota(jnp.int32, (CH, LANES), 1) == 0
            for first in (0, PART):
                s, d = (slice(first + at, first + at + LANES) for at in moved)
                w_ref[:, d] = jnp.where(lane0, w_ref[:, s], w_ref[:, d])


def cells_of(x_ref, s):
    x = x_ref[s]
    return x[:, :32].reshape(CH, LANES), x[:, 32:].reshape(CH, LANES)


UNROLL = 16


def cov_in(x_ref, m_ref, rhs_ref, w_ref, acc_ref, arrive):
    acc_ref[...] = jnp.zeros_like(acc_ref)

    def step(i, _):
        arrive(i)
        a, b = [], []
        for t in range(UNROLL):
            s = i * UNROLL + t
            xr, xi = cells_of(x_ref, s)
            m = jnp.broadcast_to(m_ref[pl.ds(s, 1), :].astype(jnp.bfloat16), (CH, LANES))
            xr, xi = xr * m, xi * m
            a.append(xr)
            b.append(xi)
        a, b = jnp.concatenate(a, 1), jnp.concatenate(b, 1)
        both = jnp.concatenate([a, b], 1)
        across = (((1,), (1,)), ((), ()))
        acc_ref[:CH] += lax.dot_general(both, both, across, preferred_element_type=jnp.float32)
        acc_ref[CH:] += lax.dot_general(b, a, across, preferred_element_type=jnp.float32)
        return 0

    lax.fori_loop(0, CELLS // LANES // UNROLL, step, 0)
    re = acc_ref[:CH] * (1.0 / CELLS)
    im = (acc_ref[CH:] - jnp.transpose(acc_ref[CH:])) * (1.0 / CELLS)
    diag = lax.broadcasted_iota(jnp.int32, (CH, CH), 0) == lax.broadcasted_iota(jnp.int32, (CH, CH), 1)
    loading = 0.1 * jnp.sum(jnp.where(diag, re, 0.0), keepdims=True) / CH + 1e-5
    w_ref[:, :CH] = re + jnp.where(diag, loading, 0.0)
    w_ref[:, CH:PART] = rhs_ref[0]
    w_ref[:, PART : PART + CH] = im
    w_ref[:, PART + CH :] = rhs_ref[1]
    return loading


def beams_out(x_ref, m_ref, w_ref, loading, out_ref):
    wr, wi = (
        jnp.transpose(w_ref[:, o : o + LANES])[:1].astype(jnp.bfloat16).astype(jnp.float32) for o in (LANES, PART + LANES)
    )
    first = lax.broadcasted_iota(jnp.int32, (8, CH), 0)
    left = jnp.where(first == 0, wr, jnp.where(first == 1, -wi, 0.0))
    right = jnp.where(first == 0, wi, jnp.where(first == 1, wr, 0.0))
    lhs = jnp.concatenate([left, right], 1).astype(jnp.bfloat16)

    def step(i, p):
        x = []
        for t in range(UNROLL):
            x.append(jnp.concatenate(cells_of(x_ref, i * UNROLL + t), 0))
        raw = jnp.dot(lhs, jnp.concatenate(x, 1), preferred_element_type=jnp.float32)
        for t in range(UNROLL):
            s = i * UNROLL + t
            r = raw[:, LANES * t : LANES * t + LANES]
            out_ref[s] = r[:2]
            p = p + r * r * m_ref[pl.ds(s, 1), :]
        return p

    p = lax.fori_loop(0, CELLS // LANES // UNROLL, step, jnp.zeros((8, LANES), jnp.float32))
    sq = jnp.sum(wr * wr + wi * wi, keepdims=True)
    power = jnp.sum(p, keepdims=True) * (1.0 / CELLS) + loading * sq
    out_ref[...] = out_ref[...] * lax.rsqrt(power).reshape(1, 1, 1)


def bin_kernel(x_hbm, m_ref, rhs_ref, out_ref, x_ref, w_ref, acc_ref, s_ref, in_sem):
    def fetch(i):
        rows = pl.ds(i * UNROLL, UNROLL)
        return pltpu.make_async_copy(x_hbm.at[rows], x_ref.at[rows], in_sem.at[i])

    for i in range(CELLS // LANES // UNROLL):
        fetch(i).start()
    loading = cov_in(x_ref, m_ref, rhs_ref, w_ref, acc_ref, lambda i: fetch(i).wait())
    solve_in(w_ref, s_ref)
    beams_out(x_ref, m_ref, w_ref, loading, out_ref)


def one_bin(x, m, rhs):
    return pl.pallas_call(
        bin_kernel,
        out_shape=jax.ShapeDtypeStruct((CELLS // LANES, 2, LANES), jnp.float32),
        in_specs=[pl.BlockSpec(memory_space=HBM)] + [pl.BlockSpec(memory_space=pltpu.VMEM)] * 2,
        out_specs=pl.BlockSpec(memory_space=pltpu.VMEM),
        scratch_shapes=[
            pltpu.VMEM(x.shape, x.dtype),
            pltpu.VMEM((CH, 2 * PART), jnp.float32),
            pltpu.VMEM((2 * CH, CH), jnp.float32),
            pltpu.VMEM((2 * SLOTS, 8, LANES), jnp.float32),
            pltpu.SemaphoreType.DMA((CELLS // LANES // UNROLL,)),
        ],
        compiler_params=pltpu.CompilerParams(vmem_limit_bytes=VMEM_LIMIT),
        name="one_bin",
    )(x, m, rhs)


GROUP = 16
IN_STRIDE = 24
OUT_STRIDE = 40


def doppler_rows(period, bins, blocks):
    pulse_index = np.arange(period, dtype=np.int32)
    bin_index = np.arange(bins, dtype=np.int32).reshape(blocks, -1).T.reshape(-1)
    turn_count = bin_index[:, None] * pulse_index[None, :] % period
    phase_angle = np.float32(2.0 * math.pi / period) * turn_count.astype(np.float32)
    window_taper = np.float32(0.54) - np.float32(0.46) * np.cos(
        np.float32(2.0 * math.pi / (period - 1)) * pulse_index.astype(np.float32)
    )
    cosine = window_taper * np.cos(phase_angle)
    sine_part = window_taper * np.sin(phase_angle)
    return np.concatenate(
        [np.concatenate([cosine, sine_part], 1), np.concatenate([-sine_part, cosine], 1)], 0
    ).astype(ml_dtypes.bfloat16)


PIECES = 2


def transform_kernel(
    table_hbm, x_hbm, out_hbm, table_ref, raw_ref, wide_ref, back_ref, out_ref, table_sem, in_sem, out_sem
):
    parts, pulses, channels = x_hbm.shape[:3]
    depth, bins, groups = parts * pulses, out_hbm.shape[0], channels // GROUP
    step = depth // PIECES

    def fetch(g, i):
        k, first = divmod(i * step, pulses)
        return pltpu.make_async_copy(
            x_hbm.at[k, pl.ds(first, step), pl.ds(GROUP * g, GROUP), :],
            raw_ref.at[g, pl.ds(step * i, step)],
            in_sem.at[g, i],
        )

    def send(g, k):
        return pltpu.make_async_copy(
            out_ref.at[g, k], out_hbm.at[:, k, pl.ds(GROUP * g, GROUP), :], out_sem.at[g, k]
        )

    table_copy = pltpu.make_async_copy(table_hbm, table_ref, table_sem)
    for i in range(PIECES):
        fetch(0, i).start()
    table_copy.start()
    flat = wide_ref.reshape((depth + 1) * IN_STRIDE, LANES)
    bflat = back_ref.reshape((bins + 1) * OUT_STRIDE, LANES)
    for g in range(groups):
        for i in range(PIECES):
            fetch(g, i).wait()
            if g + 1 < groups:
                fetch(g + 1, i).start()
            rows = pl.ds(step * i, step)
            wide_ref[rows, :GROUP] = raw_ref[g, rows].astype(jnp.float32)
        if g == 0:
            table_copy.wait()
        for c in range(0, GROUP, 2):
            x = [flat[pl.ds(c + i, depth, stride=IN_STRIDE), :].astype(jnp.bfloat16) for i in range(2)]
            y = jnp.dot(table_ref[...], jnp.concatenate(x, 1), preferred_element_type=jnp.float32)
            for k in range(2):
                for i in range(2):
                    bflat[pl.ds(k * GROUP + c + i, bins, stride=OUT_STRIDE), :] = y[
                        bins * k : bins * k + bins, LANES * i : LANES * i + LANES
                    ]
        for k in range(2):
            out_ref[g, k] = back_ref[:bins, k * GROUP : k * GROUP + GROUP].astype(jnp.bfloat16)
            send(g, k).start()
    for g in range(groups):
        for k in range(2):
            send(g, k).wait()


def transform(pulses, bins, blocks):
    parts, period, channels, cells = pulses.shape
    table = jnp.asarray(doppler_rows(period, bins, blocks))
    groups, depth = channels // GROUP, parts * period
    return pl.pallas_call(
        transform_kernel,
        out_shape=jax.ShapeDtypeStruct((bins, 2, channels, cells), jnp.bfloat16),
        in_specs=[pl.BlockSpec(memory_space=HBM)] * 2,
        out_specs=pl.BlockSpec(memory_space=HBM),
        scratch_shapes=[
            pltpu.VMEM((2 * bins, depth), jnp.bfloat16),
            pltpu.VMEM((groups, depth, GROUP, cells), jnp.bfloat16),
            pltpu.VMEM((depth + 1, IN_STRIDE, cells), jnp.float32),
            pltpu.VMEM((bins + 1, OUT_STRIDE, cells), jnp.float32),
            pltpu.VMEM((groups, 2, bins, GROUP, cells), jnp.bfloat16),
            pltpu.SemaphoreType.DMA,
            pltpu.SemaphoreType.DMA((groups, PIECES)),
            pltpu.SemaphoreType.DMA((groups, 2)),
        ],
        compiler_params=pltpu.CompilerParams(vmem_limit_bytes=VMEM_LIMIT),
        name="transform",
    )(table, pulses)


from jax.sharding import PartitionSpec as P

NANG = 64


def steering(index, channels):
    sine_of = -0.9 + 1.8 * index.astype(jnp.float32) / (NANG - 1)
    phase_angle = math.pi * jnp.arange(channels, dtype=jnp.float32) * sine_of
    pair = jnp.stack([jnp.cos(phase_angle), jnp.sin(phase_angle)])
    return jnp.pad(pair[:, :, None], ((0, 0), (0, 0), (0, LANES - 1)))


def on_device(pulses, guard, steer_index):
    bins = steer_index.shape[0] * lax.axis_size("dop")
    spectrum = transform(pulses, bins, lax.axis_size("dop"))
    mask = 1.0 - lax.all_gather(guard, "rng", axis=0).astype(jnp.float32)
    rhs = steering(steer_index[lax.axis_index("rng")], CH)
    whole = lax.all_to_all(spectrum, ("rng", "dop"), split_axis=0, concat_axis=0, tiled=True)
    beams = one_bin(whole.reshape(CELLS // LANES, 8, 64, LANES), mask, rhs)
    return lax.all_to_all(beams, "rng", split_axis=0, concat_axis=0, tiled=True)


def solution(mesh):
    return jax.shard_map(
        on_device,
        mesh=mesh,
        in_specs=(P(None, None, "dop", "rng"), P("rng"), P("dop")),
        out_specs=P("dop", None, "rng"),
        check_vma=False,
    )
```
